512 devices in a mesh: ctx: 64 (over y, z_lo, core), head: 8 (over z_hi, x).
Axes of the slice: x: 4, y: 8, z: 8 (z_hi: 2, z_lo: 4; z = z_hi * 4 + z_lo), core: 2. Of those that a mesh axis runs over, the one named last changes fastest.
Arguments:
- hidden_in: bfloat16 [8192, 4096], P('ctx'), may hold values from -3 to 3
- positions: int32 [8192], P('ctx'), may hold values from 0 to 8191, as said below
- w_query: bfloat16 [4096, 4096], P('ctx', 'head'), may hold values from -0.5 to 0.5
- w_key: bfloat16 [4096, 1024], P('ctx', 'head'), may hold values from -0.5 to 0.5
- w_value: bfloat16 [4096, 1024], P('ctx', 'head'), may hold values from -0.5 to 0.5
- w_out: bfloat16 [4096, 4096], P('head', 'ctx'), may hold values from -0.5 to 0.5
- norm_gain: float32 [4096], replicated, may hold values from 0.1 to 1.9
Outputs:
- normed: bfloat16 [8192, 4096], P(('ctx', 'head'))
The draws below stay inside these ranges and needn't reach their ends.
Inputs may be any that keep to these rules, and one draw needn't show every extreme that they name: Each aligned block of 64 rows holds exactly the positions of that block's range of 64 rows, each once, in some order.
All inputs are finite; a program needn't handle non-finite values.
Results may differ from the reference program's by a relative error of at most 0.02.
Values may be sent and summed in bfloat16 or wider, within the bound.
A program may use at most 64 MiB of HBM per device.

```python
import jax
import jax.numpy as jnp
from jax import lax

D = 4096
QH = 32
KVH = 8
HD = 128
TOKENS = 8192
N_CTX = 64
N_HEAD = 8


def draw_hidden_in(key, part):
    key = jax.random.fold_in(key, 11)
    first = jax.random.fold_in(key, 0)
    values = 0.25 * jax.random.normal(first, (TOKENS, D), jnp.float32)
    return jnp.clip(values, -3.0, 3.0).astype(jnp.bfloat16)


def draw_positions(key, part):
    key = jax.random.fold_in(key, 23)
    rounds = TOKENS // N_CTX
    keys = jax.random.split(key, rounds)
    order = jax.vmap(lambda single: jax.random.permutation(single, N_CTX))(keys)
    base = jnp.arange(rounds, dtype=jnp.int32)[:, None] * N_CTX
    return (base + order.astype(jnp.int32)).reshape(TOKENS)


def steps_of(own_key, shape, cuts, least, largest):
    factor_of = 1.0
    for axis_at, shards_of in cuts:
        heights = jax.random.uniform(jax.random.fold_in(jax.random.fold_in(own_key, 6), axis_at), (shards_of,), jnp.float32, least / len(cuts), largest / len(cuts))
        factor_of = factor_of * jnp.repeat(jnp.exp(heights), shape[axis_at] // shards_of).reshape((-1,) + (1,) * (len(shape) - 1 - axis_at))
    return factor_of


def normal_values(stream_key, dims, width, limit, shards=(), kind=jnp.bfloat16):
    entries = jax.random.normal(stream_key, dims, jnp.float32) * width
    if len(shards) > 0:
        entries = steps_of(stream_key, dims, shards, -0.22, 0.18) * entries
    return jnp.clip(entries, min=-limit, max=limit).astype(kind)


def setup_inputs(seed: int = 0) -> dict:
    key_of = jax.random.split(jax.random.key(seed), 8)
    return {
        "hidden_in": draw_hidden_in(jax.random.fold_in(key_of[7], 71), 0),
        "positions": draw_positions(jax.random.fold_in(key_of[7], 71), 0),
        "w_query": normal_values(key_of[2], (D, QH * HD), (D // 32) ** -0.5, 0.5, ((0, 64), (1, 8))),
        "w_key": normal_values(key_of[3], (D, KVH * HD), (D // 32) ** -0.5, 0.5, ((0, 64), (1, 8))),
        "w_value": normal_values(key_of[4], (D, KVH * HD), (D // 32) ** -0.5, 0.5, ((0, 64), (1, 8))),
        "w_out": normal_values(key_of[5], (QH * HD, D), HD ** -0.5, 0.5, ((0, 8), (1, 64))),
        "norm_gain": jnp.clip(1.0 + 0.18 * jax.random.normal(key_of[6], (D,), jnp.float32), 0.1, 1.9),
    }


def rotate(values, places):
    half = HD // 2
    inverse = 500000.0 ** (-(jnp.arange(half, dtype=jnp.float32) * 2.0 / HD))
    angle = places.astype(jnp.float32)[:, None, None] * inverse[None, None, :]
    cosine = jnp.cos(angle)
    sine = jnp.sin(angle)
    first = values[..., :half]
    second = values[..., half:]
    return jnp.concatenate([first * cosine - second * sine, second * cosine + first * sine], axis=-1)

def reference(hidden_in, positions, w_query, w_key, w_value, w_out, norm_gain):
    total_rows = hidden_in.shape[0]
    ratio = QH // KVH
    query = rotate(jnp.dot(hidden_in, w_query, preferred_element_type=jnp.float32).reshape(total_rows, QH, HD), positions).astype(jnp.bfloat16)
    key = rotate(jnp.dot(hidden_in, w_key, preferred_element_type=jnp.float32).reshape(total_rows, KVH, HD), positions).astype(jnp.bfloat16)
    value = jnp.dot(hidden_in, w_value, preferred_element_type=jnp.float32).astype(jnp.bfloat16).reshape(total_rows, KVH, HD)
    grouped = query.reshape(total_rows, KVH, ratio, HD)
    key_wide = key.astype(jnp.float32)
    value_wide = value.astype(jnp.float32)
    block = min(256, total_rows)
    scale = 1.0 / jnp.sqrt(jnp.float32(HD))

    def one_block(start):
        rows = lax.dynamic_slice_in_dim(grouped, start, block, 0).astype(jnp.float32)
        places = lax.dynamic_slice_in_dim(positions, start, block, 0)
        score = jnp.einsum('qgrd,kgd->grqk', rows, key_wide) * scale
        visible = positions[None, :] <= places[:, None]
        score = jnp.where(visible[None, None], score, -1e+30)
        peak = lax.optimization_barrier(jnp.max(score, axis=-1, keepdims=True))
        weight = jnp.where(visible[None, None], jnp.exp(score - peak), 0.0)
        total = lax.optimization_barrier(jnp.sum(weight, axis=-1))
        rounded = lax.optimization_barrier(weight.astype(jnp.bfloat16)).astype(jnp.float32)
        summed = jnp.einsum('grqk,kgd->qgrd', rounded, value_wide)
        summed = summed / jnp.transpose(total, (2, 0, 1))[..., None]
        return summed.reshape(block, QH * HD).astype(jnp.bfloat16)
    starts = (jnp.arange(total_rows // block) * block).astype(jnp.int32)
    attended = lax.map(one_block, starts).reshape(total_rows, QH * HD)
    group_cols = QH * HD // N_HEAD
    mixed = jnp.zeros((total_rows, hidden_in.shape[1]), jnp.float32)
    for group in range(N_HEAD):
        part = jnp.dot(attended[:, group * group_cols:(group + 1) * group_cols], w_out[group * group_cols:(group + 1) * group_cols], preferred_element_type=jnp.float32)
        mixed = mixed + lax.optimization_barrier(part.astype(jnp.bfloat16)).astype(jnp.float32)
    residual = hidden_in.astype(jnp.float32) + mixed
    spread = lax.optimization_barrier(jnp.mean(residual * residual, axis=-1, keepdims=True))
    return (residual * lax.rsqrt(spread + 1e-05) * norm_gain).astype(jnp.bfloat16)
```

```python
import jax
import jax.numpy as jnp
from jax import lax
from jax.sharding import PartitionSpec as P

QH = 32
KVH = 8
HD = 128
NEGATIVE = -1e30


def rotate(values, places):
    half = HD // 2
    inverse = 500000.0 ** (-(jnp.arange(half, dtype=jnp.float32) * 2.0 / HD))
    angle = places.astype(jnp.float32)[:, None, None] * inverse[None, None, :]
    cosine = jnp.cos(angle)
    sine = jnp.sin(angle)
    first = values[..., :half]
    second = values[..., half:]
    return jnp.concatenate(
        [first * cosine - second * sine, second * cosine + first * sine], axis=-1
    )


def on_device(hidden_in, positions, w_query, w_key, w_value, w_out, norm_gain):
    here = lax.axis_index("ctx")
    tok = hidden_in.shape[0]
    q_cols = w_query.shape[1]
    kv_cols = w_key.shape[1]
    ratio = QH // KVH
    joined = jnp.concatenate([w_query, w_key, w_value], axis=1)
    w_all = lax.all_gather(joined, "ctx", axis=0, tiled=True)
    out_weight = lax.all_gather(w_out.T, "ctx", axis=0, tiled=True)
    full = jnp.dot(hidden_in, w_all, preferred_element_type=jnp.float32)
    turned = rotate(
        full[:, : q_cols + kv_cols].reshape(tok, -1, HD), positions
    ).astype(jnp.bfloat16)
    value = full[:, q_cols + kv_cols :].astype(jnp.bfloat16)
    key = turned[:, ratio:].reshape(tok, kv_cols)
    kv = lax.all_gather(
        jnp.concatenate([key, value], axis=1), "ctx", axis=0, tiled=True
    )
    keys, values = kv[:, :HD], kv[:, HD:]
    rows = turned[:, :ratio].transpose(1, 0, 2).reshape(ratio * tok, HD)
    score = jnp.einsum(
        "rd,kd->rk", rows, keys, preferred_element_type=jnp.float32
    ) * (1.0 / jnp.sqrt(jnp.float32(HD)))
    column = jnp.arange(keys.shape[0], dtype=jnp.int32)
    spread_places = jnp.where(
        column < here * tok, -1, jnp.where(column >= (here + 1) * tok, 1 << 30, 0)
    )
    spread_places = lax.dynamic_update_slice(spread_places, positions, (here * tok,))
    row_places = jnp.tile(positions, ratio)
    visible = spread_places[None, :] <= row_places[:, None]
    score = jnp.where(visible, score, NEGATIVE)
    peak = jnp.max(score, axis=-1, keepdims=True)
    weight = jnp.exp(score - peak)
    total = jnp.sum(weight, axis=-1, keepdims=True)
    summed = jnp.dot(
        weight.astype(jnp.bfloat16), values, preferred_element_type=jnp.float32
    )
    attended = (
        (summed / total)
        .reshape(ratio, tok, HD)
        .transpose(1, 0, 2)
        .reshape(tok, q_cols)
        .astype(jnp.bfloat16)
    )
    heads = lax.axis_size("head")
    share = tok // heads
    product = lax.dot_general(
        attended, out_weight, (((1,), (1,)), ((), ())), preferred_element_type=jnp.float32
    ).astype(jnp.bfloat16)
    mixed = lax.psum_scatter(product, "head", scatter_dimension=0, tiled=True).astype(
        jnp.float32
    )
    own_rows = lax.dynamic_slice_in_dim(
        hidden_in, lax.axis_index("head") * share, share, 0
    ).astype(jnp.float32)
    residual = own_rows + mixed
    spread = jnp.mean(residual * residual, axis=-1, keepdims=True)
    return (residual * lax.rsqrt(spread + 1e-05) * norm_gain).astype(jnp.bfloat16)


def solution(mesh):
    return jax.shard_map(
        on_device,
        mesh=mesh,
        in_specs=(
            P("ctx", None),
            P("ctx"),
            P("ctx", "head"),
            P("ctx", "head"),
            P("ctx", "head"),
            P("head", "ctx"),
            P(),
        ),
        out_specs=P(("ctx", "head"), None),
        check_vma=False,
    )
```

```python
import jax
import jax.numpy as jnp
from jax import lax
from jax.experimental import pallas as pl
from jax.experimental.pallas import tpu as pltpu
from jax.sharding import PartitionSpec as P

MESH = pl.DeviceIdType.MESH
HD = 128
ROWS = 8
LINE = 4
CHIPS = ROWS * LINE
WAVES = ROWS // 2 + LINE
O_AT = 5
NEGATIVE = -1e30
SCALE = 1.4426950408889634 / HD ** 0.5
ORDER = (3, 2, 1, 0)


class Place:
    def __init__(self):
        ctx = lax.axis_index("ctx")
        head = lax.axis_index("head")
        self.core = ctx % 2
        self.z = (ctx // 2) % LINE
        self.y = ctx // (2 * LINE)
        self.x = head % 4
        self.zh = head // 4
        self.chip = ctx // 2
        self.ctx = ctx
        self.head = head

    def at(self, y, z, core):
        return ((y * LINE + z) * 2 + core, self.head)

    def sibling(self):
        return (self.chip * 2 + 1 - self.core, self.head)

    def up(self):
        return self.at((self.y + 1) % ROWS, self.z, self.core)

    def down(self):
        return self.at((self.y + ROWS - 1) % ROWS, self.z, self.core)

    def right(self):
        return self.at(self.y, jnp.minimum(self.z + 1, LINE - 1), self.core)

    def left(self):
        return self.at(self.y, jnp.maximum(self.z - 1, 0), self.core)

    def across(self, steps):
        return (self.ctx, self.zh * 4 + (self.x + 4 + steps) % 4)

    def far(self):
        return (self.ctx, (1 - self.zh) * 4 + self.x)

    def order(self, i):
        z = self.z
        if i == 0:
            return z
        a = (1, 0, 3, 2)
        b = (2, 2, 1, 1)
        c = (3, 3, 0, 0)
        t = (a, b, c)[i - 1]
        return jnp.where(z == 0, t[0], jnp.where(z == 1, t[1], jnp.where(z == 2, t[2], t[3])))


class Gather:
    def __init__(self, place, first, last, sems, relay=None):
        self.p = place
        self.first, self.last = first, last
        self.relay = relay
        self.recv, self.by, self.bz, self.ay, self.az = sems

    @staticmethod
    def scratch():
        dma = pltpu.SemaphoreType.DMA
        return [dma((2, CHIPS)), dma((2, CHIPS)), dma((2, LINE)), dma((2, ROWS)), dma((2, CHIPS))]

    def row(self, g):
        d = (g + 1) // 2
        core = self.p.core
        up = jnp.logical_and(g % 2 == 1, jnp.logical_or(g < 7, core == 0))
        return jnp.where(up, self.p.y + ROWS - d, self.p.y + d) % ROWS

    def sends(self, g, i, slot, zq):
        p = self.p
        core = p.core
        up = (g == 0) | (g == 1) | (g == 3) | ((g == 5) & (core == 0))
        down = (g == 0) | (g == 2) | (g == 4) | ((g == 6) & (core == 1))
        if i == 0:
            right, left = p.z < LINE - 1, p.z > 0
        else:
            right = (zq < p.z) & (p.z < LINE - 1)
            left = (zq > p.z) & (p.z > 0)
        s = g * LINE + i

        def copy(part, sem, device):
            ref = (self.first, self.last)[part].at[slot]
            return pltpu.make_async_remote_copy(
                src_ref=ref, dst_ref=ref, send_sem=sem, recv_sem=self.recv.at[part, slot],
                device_id=device, device_id_type=MESH)

        out = []
        out.append((up, lambda: copy(0, self.by.at[0, s], p.up())))
        out.append((down, lambda: copy(0, self.by.at[1, s], p.down())))
        out.append(((g == 0) & right, lambda: copy(0, self.bz.at[0, i], p.right())))
        out.append(((g == 0) & left, lambda: copy(0, self.bz.at[1, i], p.left())))
        if i == 0:
            out.append((up, lambda: copy(1, self.ay.at[0, g], p.up())))
            out.append((down, lambda: copy(1, self.ay.at[1, g], p.down())))
        out.append((right, lambda: copy(1, self.az.at[0, s], p.right())))
        out.append((left, lambda: copy(1, self.az.at[1, s], p.left())))
        return out

    def arrive(self, part, slot):
        ref = (self.first, self.last)[part].at[slot]
        pltpu.make_async_remote_copy(
            src_ref=ref, dst_ref=ref, send_sem=self.recv.at[part, slot],
            recv_sem=self.recv.at[part, slot], device_id=self.p.up(), device_id_type=MESH).wait_recv()

    def step(self, g, i):
        zq = self.p.order(i)
        slot = self.row(g) * LINE + zq

        def wait(part):
            if i == 0:
                pl.when(g > 0)(lambda: self.arrive(part, slot))
            else:
                self.arrive(part, slot)

        out = self.sends(g, i, slot, zq)
        wait(0)
        for cond, make in out[:4]:
            pl.when(cond)(lambda make=make: make().start())
        if self.relay is not None:
            self.relay(0, slot).start()
        wait(1)
        for cond, make in out[4:]:
            pl.when(cond)(lambda make=make: make().start())
        if self.relay is not None:
            self.relay(1, slot).start()

    def wave(self, t):
        for i in ORDER:
            d = t - i
            pl.when((d >= 1) & (d <= 4))(lambda d=d, i=i: self.step(2 * d - 1, i))
            pl.when((d >= 0) & (d <= 3))(lambda d=d, i=i: self.step(2 * d, i))

    def drain(self):
        def one(g, _):
            for i in range(LINE):
                zq = self.p.order(i)
                slot = self.row(g) * LINE + zq
                for cond, make in self.sends(g, i, slot, zq):
                    pl.when(cond)(lambda make=make: make().wait_send())
            return 0
        lax.fori_loop(0, ROWS, one, 0)


def entry(p, extra=()):
    bar = pltpu.get_barrier_semaphore()
    always = [p.sibling(), p.up(), p.down()] + list(extra)
    for d in always:
        pl.semaphore_signal(bar, inc=1, device_id=d, device_id_type=MESH)

    @pl.when(p.z < LINE - 1)
    def _():
        pl.semaphore_signal(bar, inc=1, device_id=p.right(), device_id_type=MESH)

    @pl.when(p.z > 0)
    def _():
        pl.semaphore_signal(bar, inc=1, device_id=p.left(), device_id_type=MESH)

    ends = (p.z == 0).astype(jnp.int32) + (p.z == LINE - 1).astype(jnp.int32)
    pl.semaphore_wait(bar, len(always) + 2 - ends)


def remote(src, dst, send, recv, device):
    return pltpu.make_async_remote_copy(
        src_ref=src, dst_ref=dst, send_sem=send, recv_sem=recv, device_id=device, device_id_type=MESH)


def load_inputs(p, x_ref, wq_ref, wk_ref, wv_ref, aux_ref, hid, aux, wf, wl, loc, snd, rcv):
    core, chip = p.core, p.chip
    tok = x_ref.shape[0]
    depth = wq_ref.shape[0]
    half = wq_ref.shape[1] // 2
    other = 1 - core
    mine = pl.ds(pl.multiple_of(core * half, half), half)
    theirs = pl.ds(pl.multiple_of(other * half, half), half)
    span = pl.ds(pl.multiple_of(core * depth, depth), depth)
    rows = pl.ds(pl.multiple_of(core * tok, tok), tok)
    sib = p.sibling()
    slot_f = wf.at[chip, span]
    slot_l = wl.at[chip, span]
    rem = [
        remote(wq_ref.at[:, theirs], slot_f, snd.at[0], rcv.at[0], sib),
        None,
        remote(x_ref, hid.at[rows], snd.at[2], rcv.at[2], sib),
        remote(aux_ref, aux.at[rows], snd.at[3], rcv.at[3], sib),
    ]
    own = [
        pltpu.make_async_copy(wq_ref.at[:, mine], slot_f, loc.at[0]),
        None,
        pltpu.make_async_copy(x_ref, hid.at[rows], loc.at[2]),
        pltpu.make_async_copy(aux_ref, aux.at[rows], loc.at[3]),
    ]

    @pl.when(core == 0)
    def _():
        remote(wv_ref, slot_l, snd.at[1], rcv.at[1], sib).start()
        pltpu.make_async_copy(wk_ref, slot_l, loc.at[1]).start()

    @pl.when(core == 1)
    def _():
        remote(wk_ref, slot_l, snd.at[1], rcv.at[1], sib).start()
        pltpu.make_async_copy(wv_ref, slot_l, loc.at[1]).start()

    rem[1] = remote(wk_ref, slot_l, snd.at[1], rcv.at[1], sib)
    own[1] = pltpu.make_async_copy(wk_ref, slot_l, loc.at[1])
    for k in (0, 2, 3):
        rem[k].start()
        own[k].start()
    return rem, own


def wait_inputs(rem, own, ks):
    for k in ks:
        own[k].wait()
        rem[k].wait_send()
        rem[k].wait_recv()


def turn(u, cosine, sine):
    return u * cosine + pltpu.roll(u, 64, 1) * sine


def angles(positions):
    half = HD // 2
    inverse = 500000.0 ** (-(jnp.arange(half, dtype=jnp.float32) * 2.0 / HD))
    angle = positions.astype(jnp.float32)[:, None] * inverse[None, :]
    cosine, sine = jnp.cos(angle), jnp.sin(angle)
    return jnp.concatenate([cosine, cosine, -sine, sine], axis=1)

def attend(q_ref, m_ref, l_ref, acc_ref, keys, values, visible=None):
    rows = q_ref.shape[0] // 2
    for h in range(2):
        at = pl.ds(h * rows, rows)
        score = lax.dot_general(q_ref[at], keys, (((1,), (1,)), ((), ())), preferred_element_type=jnp.float32)
        if visible is not None:
            score = jnp.where(visible, score, NEGATIVE)
        before = m_ref[at]
        peak = jnp.maximum(before, jnp.max(score, axis=1, keepdims=True))
        fade = jnp.exp2((before - peak) * SCALE)
        weight = jnp.exp2((score - peak) * SCALE)
        m_ref[at] = peak
        l_ref[at] = l_ref[at] * fade + jnp.sum(weight, axis=1, keepdims=True)
        acc_ref[at] = acc_ref[at] * fade + jnp.dot(
            weight.astype(jnp.bfloat16), values, preferred_element_type=jnp.float32)


def block_kernel(x_ref, wq_ref, wk_ref, wv_ref, wo_ref, aux_ref, gain_ref, out_ref,
                 hid, aux, wf, wl, acc_f, acc_l, kvf, kvl, of, ol, qs, m_ref, l_ref, acc, att,
                 part, xin, zout, zin, fin, tin, loc, snd, rcv, sib_s, sib_r, att_sem, x_s, x_r, z_s, z_r, t_s, t_r, *gsems):
    p = Place()
    core, chip = p.core, p.chip
    tok = x_ref.shape[0]
    sib = p.sibling()
    entry(p, (p.across(1), p.across(-1), p.across(2), p.far()))
    rem, own = load_inputs(p, x_ref, wq_ref, wk_ref, wv_ref, aux_ref, hid, aux, wf, wl, loc, snd, rcv)
    wide = of.shape[2]
    o_own = [pltpu.make_async_copy(wo_ref.at[:, pl.ds(0, wide)], of.at[chip], loc.at[4]),
             pltpu.make_async_copy(wo_ref.at[:, pl.ds(wide, ol.shape[2])], ol.at[chip], loc.at[5])]
    for c in o_own:
        c.start()
    n = len(gsems) // 3
    g_w = Gather(p, wf, wl, gsems[:n])
    g_o = Gather(p, of, ol, gsems[n:2 * n])

    def relay(part_at, slot):
        ref = (kvf, kvl)[part_at].at[core, slot]
        return remote(ref, ref, sib_s.at[part_at, slot], sib_r.at[part_at, slot], sib)

    g_kv = Gather(p, kvf.at[core], kvl.at[core], gsems[2 * n:], relay)
    wait_inputs(rem, own, (0, 1))
    acc_f[...] = jnp.zeros_like(acc_f)
    acc_l[...] = jnp.zeros_like(acc_l)

    def project(t, _):
        g_w.wave(t)

        @pl.when(t == O_AT)
        def _():
            for c in o_own:
                c.wait()
        g_o.wave(t - O_AT)
        d = t - (LINE - 1)

        def use(g):
            row = g_w.row(g)
            depth = LINE * 128
            left = hid[:, pl.ds(pl.multiple_of(row * depth, depth), depth)]
            at = pl.ds(pl.multiple_of(row * LINE, LINE), LINE)
            acc_f[...] += jnp.dot(left, wf[at].reshape(depth, wf.shape[2]), preferred_element_type=jnp.float32)
            acc_l[...] += jnp.dot(left, wl[at].reshape(depth, wl.shape[2]), preferred_element_type=jnp.float32)

        @pl.when(d == 0)
        def _():
            wait_inputs(rem, own, (2, 3))

        pl.when(d >= 1)(lambda: use(2 * d - 1))
        pl.when((d >= 0) & (d <= 3))(lambda: use(2 * d))
        return 0

    lax.fori_loop(0, WAVES, project, 0)

    cosine, sine = aux[:, 0:HD], aux[:, HD:2 * HD]
    last = acc_l[...]
    own_kv = jnp.where(core == 0, turn(last, cosine, sine), last).astype(jnp.bfloat16)
    cut = kvf.shape[2]
    kvf[core, chip] = own_kv[:cut]
    kvl[core, chip] = own_kv[cut:]
    for h in range(2):
        qs[pl.ds(2 * tok * h, 2 * tok)] = turn(acc_f[:, h * HD:(h + 1) * HD], cosine, sine).astype(jnp.bfloat16)
    m_ref[...] = jnp.full_like(m_ref, NEGATIVE)
    l_ref[...] = jnp.zeros_like(l_ref)
    acc[...] = jnp.zeros_like(acc)

    def arrived(slot):
        for part_at in range(2):
            ref = (kvf, kvl)[part_at].at[1 - core, slot]
            remote(ref, ref, sib_s.at[part_at, slot], sib_r.at[part_at, slot], sib).wait_recv()

    def block(kind, start, count):
        at = pl.ds(start, count)
        return jnp.concatenate([kvf[kind, at].reshape(count * cut, HD),
                                kvl[kind, at].reshape(count * (2 * tok - cut), HD)], axis=0)

    def look(t, _):
        g_kv.wave(t)
        g_o.wave(t + WAVES - O_AT)
        d = t - (LINE - 1)

        @pl.when(t == 0)
        def _():
            arrived(chip)
            vis = aux[:, 2 * HD:3 * HD]
            visible = jnp.concatenate([
                jnp.concatenate([vis[:tok], jnp.zeros_like(vis[:tok])], axis=1),
                jnp.concatenate([jnp.ones_like(vis[tok:]), vis[tok:]], axis=1)], axis=0) > 0.5
            attend(qs, m_ref, l_ref, acc, block(0, chip, 1), block(1, chip, 1), visible)

        @pl.when(d == 0)
        def _():
            def one(z, _):
                slot = p.y * LINE + z
                pl.when(z != p.z)(lambda: arrived(slot))
                pl.when(z < p.z)(lambda: attend(qs, m_ref, l_ref, acc, block(0, slot, 1), block(1, slot, 1)))
                return 0
            lax.fori_loop(0, LINE, one, 0)

        def use(g, _):
            @pl.when((g >= 1) & (g < ROWS))
            def _():
                row = g_kv.row(g)
                start = pl.multiple_of(row * LINE, LINE)
                for i in range(LINE):
                    arrived(start + i)
                pl.when(row < p.y)(lambda: attend(qs, m_ref, l_ref, acc, block(0, start, LINE), block(1, start, LINE)))
            return 0

        @pl.when(d >= 1)
        def _():
            lax.fori_loop(2 * d - 1, 2 * d + 1, use, 0)
        return 0

    lax.fori_loop(0, WAVES, look, 0)

    done = (acc[...] / l_ref[...]).astype(jnp.bfloat16)
    share = tok // 8
    for h in range(2):
        for xt in range(4):
            for zt in range(2):
                for c in range(2):
                    src = h * 2 * tok + c * tok + (zt * 4 + xt) * share
                    dst = (xt * 4 + zt * 2 + c) * share
                    att[core, dst:dst + share, h * HD:(h + 1) * HD] = done[src:src + share]
    swap = remote(att.at[core], att.at[core], att_sem.at[0], att_sem.at[1], sib)
    swap.start()
    swap.wait()

    span = LINE * 64
    piece = 4 * share
    wide_chunk = 2 * span

    def x_copies(c):
        cols = pl.ds(pl.multiple_of(c * wide_chunk, wide_chunk), wide_chunk)
        out = []
        for k, step in enumerate((1, 3, 2)):
            to = (p.x + step) % 4
            out.append(remote(part.at[to, :, cols], xin.at[k, :, cols], x_s.at[k, c], x_r.at[k, c], p.across(step)))
        return out

    def z_copy(c):
        cols = pl.ds(pl.multiple_of(c * wide_chunk, wide_chunk), wide_chunk)
        return remote(zout.at[:, cols], zin.at[:, cols], z_s.at[c], z_r.at[c], p.far())

    def t_copy(c):
        cols = pl.ds(pl.multiple_of(c * wide_chunk, wide_chunk), wide_chunk)
        return remote(fin.at[1 - core, :, cols], tin.at[:, cols], t_s.at[c], t_r.at[c], sib)

    def produce(c, _):
        for half in range(2):
            r = 2 * c + half
            at = pl.ds(pl.multiple_of(r * LINE, LINE), LINE)
            nt = (((1,), (1,)), ((), ()))
            left = jnp.concatenate([att[0], att[1]], axis=1)
            prod = lax.dot_general(left[:, :wide], of[at].reshape(span, wide), nt, preferred_element_type=jnp.float32)
            prod += lax.dot_general(left[:, wide:], ol[at].reshape(span, ol.shape[2]), nt, preferred_element_type=jnp.float32)
            part[:, :, pl.ds(pl.multiple_of(r * span, span), span)] = prod.astype(jnp.bfloat16).reshape(4, piece, span)
        for cp in x_copies(c):
            cp.start()
        return 0

    lax.fori_loop(0, ROWS // 2, produce, 0)

    def merge_x(c, _):
        cols = pl.ds(pl.multiple_of(c * wide_chunk, wide_chunk), wide_chunk)
        for cp in x_copies(c):
            cp.wait_recv()
        half = piece // 2

        def summed(z):
            at = pl.ds(pl.multiple_of(z * half, half), half)
            f = lambda v: v.astype(jnp.float32)
            return f(part[p.x, at, cols]) + f(xin[0, at, cols]) + f(xin[1, at, cols]) + f(xin[2, at, cols])

        zout[:, cols] = summed(1 - p.zh).astype(jnp.bfloat16)
        z_copy(c).start()
        fin[:, :, cols] = summed(p.zh).reshape(2, share, wide_chunk)
        return 0

    lax.fori_loop(0, ROWS // 2, merge_x, 0)

    def merge_z(c, _):
        cols = pl.ds(pl.multiple_of(c * wide_chunk, wide_chunk), wide_chunk)
        z_copy(c).wait_recv()
        fin[:, :, cols] += zin[:, cols].astype(jnp.float32).reshape(2, share, wide_chunk)
        t_copy(c).start()
        return 0

    lax.fori_loop(0, ROWS // 2, merge_z, 0)

    def merge_t(c, _):
        t_copy(c).wait_recv()
        return 0

    lax.fori_loop(0, ROWS // 2, merge_t, 0)
    mine, theirs = fin[core], tin[...]
    even = jnp.where(core == 0, mine, theirs)
    odd = jnp.where(core == 0, theirs, mine)
    low = lax.broadcasted_iota(jnp.int32, (share, HD), 1) < HD // 2
    at = pl.ds(pl.multiple_of(core * tok + p.head * share, share), share)
    square = jnp.zeros((share, 1), jnp.float32)
    tiles = []
    for m in range(CHIPS // 2):
        a, b = even[:, m * HD:(m + 1) * HD], odd[:, m * HD:(m + 1) * HD]
        pair = (jnp.where(low, a, pltpu.roll(b, 64, 1)), jnp.where(low, pltpu.roll(a, 64, 1), b))
        for k in range(2):
            cols = pl.ds((2 * m + k) * HD, HD)
            value = pair[k] + hid[at, cols].astype(jnp.float32)
            square += jnp.sum(value * value, axis=1, keepdims=True)
            tiles.append(value)
    norm = lax.rsqrt(square * (1.0 / (CHIPS * HD)) + 1e-05)
    for m in range(CHIPS):
        cols = pl.ds(m * HD, HD)
        out_ref[:, cols] = (tiles[m] * norm * gain_ref[:, cols]).astype(jnp.bfloat16)

    g_w.drain()
    g_o.drain()
    g_kv.drain()

    def rest(c, _):
        for cp in x_copies(c):
            cp.wait_send()
        z_copy(c).wait_send()
        t_copy(c).wait_send()
        return 0

    lax.fori_loop(0, ROWS // 2, rest, 0)

    def relays(slot, _):
        for part_at in range(2):
            relay(part_at, slot).wait_send()
        return 0

    lax.fori_loop(0, CHIPS, relays, 0)


def whole(x, wq, wk, wv, wo, aux, gain):
    tok = x.shape[0]
    width = x.shape[1]
    dma = pltpu.SemaphoreType.DMA
    anyspec = pl.BlockSpec(memory_space=pl.ANY)
    vm = pl.BlockSpec(memory_space=pltpu.VMEM)
    bf, f32 = jnp.bfloat16, jnp.float32
    share = tok // 8
    half = width // 2
    return pl.pallas_call(
        block_kernel,
        out_shape=jax.ShapeDtypeStruct((share, width), bf),
        in_specs=[anyspec] * 6 + [vm],
        out_specs=vm,
        scratch_shapes=[
            pltpu.VMEM((2 * tok, width), bf),
            pltpu.VMEM((2 * tok, aux.shape[1]), f32),
            pltpu.VMEM((CHIPS, 128, 256), bf),
            pltpu.VMEM((CHIPS, 128, 128), bf),
            pltpu.VMEM((2 * tok, 256), f32),
            pltpu.VMEM((2 * tok, 128), f32),
            pltpu.VMEM((2, CHIPS, 192, HD), bf),
            pltpu.VMEM((2, CHIPS, 64, HD), bf),
            pltpu.VMEM((CHIPS, 64, 384), bf),
            pltpu.VMEM((CHIPS, 64, 128), bf),
            pltpu.VMEM((4 * tok, HD), bf),
            pltpu.VMEM((4 * tok, 1), f32),
            pltpu.VMEM((4 * tok, 1), f32),
            pltpu.VMEM((4 * tok, HD), f32),
            pltpu.VMEM((2, 2 * tok, 256), bf),
            pltpu.VMEM((4, 4 * share, half), bf),
            pltpu.VMEM((3, 4 * share, half), bf),
            pltpu.VMEM((2 * share, half), bf),
            pltpu.VMEM((2 * share, half), bf),
            pltpu.VMEM((2, share, half), f32),
            pltpu.VMEM((share, half), f32),
            dma((6,)), dma((4,)), dma((4,)),
            dma((2, CHIPS)), dma((2, CHIPS)), dma((2,)),
            dma((3, 4)), dma((3, 4)), dma((4,)), dma((4,)), dma((4,)), dma((4,)),
        ] + Gather.scratch() * 3,
        compiler_params=pltpu.CompilerParams(collective_id=0, has_side_effects=True, vmem_limit_bytes=56 << 20),
        name="block",
    )(x, wq, wk, wv, wo, aux, gain)


def on_device(hidden_in, positions, w_query, w_key, w_value, w_out, norm_gain):
    visible = (positions[None, :] <= positions[:, None]).astype(jnp.float32)
    aux = jnp.concatenate([angles(positions), visible], axis=1)
    return whole(hidden_in, w_query, w_key, w_value, w_out.T, aux, norm_gain.reshape(1, -1))


def solution(mesh):
    return jax.shard_map(
        on_device,
        mesh=mesh,
        in_specs=(P("ctx", None), P("ctx"), P("ctx", "head"), P("ctx", "head"), P("ctx", "head"), P("head", "ctx"), P()),
        out_specs=P(("ctx", "head"), None),
        check_vma=False,
    )
```

```python
import jax
import jax.numpy as jnp
from jax import lax
from jax.experimental import pallas as pl
from jax.experimental.pallas import tpu as pltpu
from jax.sharding import PartitionSpec as P

MESH = pl.DeviceIdType.MESH
HD = 128
ROWS = 8
LINE = 4
CHIPS = ROWS * LINE
ROUNDS = ROWS // 2 + 2
USE_AT = 2
STEPS = ROUNDS + USE_AT - 1
O_BEGIN = 0
O_PLAN = ((6, 1), (12, 2), (13, 3), (14, 4), (15, 5))
MERGE_AT = 2
NEGATIVE = -1e30
SCALE = 1.4426950408889634 / HD ** 0.5


class Place:
    def __init__(self):
        ctx = lax.axis_index("ctx")
        head = lax.axis_index("head")
        self.core = ctx % 2
        self.z = (ctx // 2) % LINE
        self.y = ctx // (2 * LINE)
        self.x = head % 4
        self.zh = head // 4
        self.chip = ctx // 2
        self.ctx = ctx
        self.head = head

    def at(self, y, z, core):
        return ((y * LINE + z) * 2 + core, self.head)

    def sibling(self):
        return (self.chip * 2 + 1 - self.core, self.head)

    def up(self):
        return self.at((self.y + 1) % ROWS, self.z, self.core)

    def down(self):
        return self.at((self.y + ROWS - 1) % ROWS, self.z, self.core)

    def across(self, steps):
        return (self.ctx, self.zh * 4 + (self.x + 4 + steps) % 4)

    def far(self, core):
        return (self.chip * 2 + core, (1 - self.zh) * 4 + self.x)

    def order(self, i):
        z = self.z
        if i == 0:
            return z
        a = (1, 0, 3, 2)
        b = (2, 2, 1, 1)
        c = (3, 3, 0, 0)
        t = (a, b, c)[i - 1]
        return jnp.where(z == 0, t[0], jnp.where(z == 1, t[1], jnp.where(z == 2, t[2], t[3])))


class Gather:
    def __init__(self, place, buf, cut, sems):
        self.p = place
        self.buf, self.cut = buf, cut
        self.rf, self.ly, self.lz, self.out = sems

    @staticmethod
    def scratch():
        dma = pltpu.SemaphoreType.DMA
        return [dma((CHIPS,)), dma((ROWS,)), dma((ROWS,)), dma((1,))]

    def row(self, g):
        d = (g + 1) // 2
        up = jnp.logical_and(g % 2 == 1, jnp.logical_or(g < 7, self.p.core == 0))
        return jnp.where(up, self.p.y + ROWS - d, self.p.y + d) % ROWS

    def first(self, slot):
        return self.buf.at[slot, pl.ds(0, self.cut)]

    def last(self, slot):
        return self.buf.at[slot, pl.ds(self.cut, self.buf.shape[1] - self.cut)]

    def copy(self, ref, sem, device):
        return remote(ref, ref, self.out.at[0], sem, device)

    def onward(self, g):
        core = self.p.core
        return ((g == 1) | (g == 3) | ((g == 5) & (core == 0)),
                (g == 2) | (g == 4) | ((g == 6) & (core == 1)))

    def along(self, make, g):
        up, down = self.onward(g)

        @pl.when(up)
        def _():
            make(self.p.up()).start()

        @pl.when(down)
        def _():
            make(self.p.down()).start()

    def line(self, make):
        for i in range(1, LINE):
            make(self.p.at(self.p.y, self.p.order(i), self.p.core)).start()

    def begin(self):
        p = self.p
        slot = p.chip
        self.line(lambda dev: self.copy(self.first(slot), self.rf.at[slot], dev))
        for dev in (p.up(), p.down()):
            self.copy(self.last(slot), self.ly.at[p.y], dev).start()
            self.copy(self.first(slot), self.rf.at[slot], dev).start()
        self.line(lambda dev: self.copy(self.last(slot), self.lz.at[p.y], dev))

    def near(self, g):
        row = self.row(g)
        slot = row * LINE + self.p.z
        here = self.copy(self.last(slot), self.ly.at[row], self.p.up())
        here.wait_recv()
        self.along(lambda dev: self.copy(self.last(slot), self.ly.at[row], dev), g)
        self.line(lambda dev: self.copy(self.last(slot), self.lz.at[row], dev))
        self.pass_on(g, slot)

    def pass_on(self, g, slot):
        make = lambda dev: self.copy(self.first(slot), self.rf.at[slot], dev)
        make(self.p.up()).wait_recv()
        self.along(make, g)

    def others(self, g):
        row = self.row(g)
        for i in range(1, LINE):
            self.pass_on(g, row * LINE + self.p.order(i))

    def line_arrived(self, row):
        three = self.buf.at[pl.ds(0, LINE - 1), pl.ds(self.cut, self.buf.shape[1] - self.cut)]
        self.copy(three, self.lz.at[row], self.p.up()).wait_recv()

    def round(self, t):
        for g in (2 * t - 1, 2 * t):
            pl.when((g >= 1) & (g < ROWS))(lambda g=g: self.near(g))

        @pl.when(t == 1)
        def _():
            for i in range(1, LINE):
                slot = self.p.y * LINE + self.p.order(i)
                make = lambda dev: self.copy(self.first(slot), self.rf.at[slot], dev)
                make(self.p.up()).wait_recv()
                make(self.p.up()).start()
                make(self.p.down()).start()

        for g in (2 * t - 3, 2 * t - 2):
            pl.when((g >= 1) & (g < ROWS))(lambda g=g: self.others(g))

    def drain(self):
        sent = self.buf.at[pl.ds(0, CHIPS - 1)]
        self.copy(sent, self.ly.at[0], self.p.up()).wait_send()


def remote(src, dst, send, recv, device):
    return pltpu.make_async_remote_copy(
        src_ref=src, dst_ref=dst, send_sem=send, recv_sem=recv, device_id=device, device_id_type=MESH)


def entry(p):
    bar = pltpu.get_barrier_semaphore()
    devices = [p.far(p.core), p.far(1 - p.core), p.across(2)] + [p.at(p.y, p.order(i), p.core) for i in range(LINE - 1, 0, -1)]
    devices += [p.across(1), p.across(-1), p.up(), p.down(), p.sibling()]
    for d in devices:
        pl.semaphore_signal(bar, inc=1, device_id=d, device_id_type=MESH)
    pl.semaphore_wait(bar, len(devices))


def load_inputs(p, x_ref, wq_ref, wk_ref, wv_ref, aux_ref, hid, aux, wall, loc, snd, rcv):
    core, chip = p.core, p.chip
    tok = x_ref.shape[0]
    depth = wq_ref.shape[0]
    half = wq_ref.shape[1] // 2
    other = 1 - core
    mine = pl.ds(pl.multiple_of(core * half, half), half)
    theirs = pl.ds(pl.multiple_of(other * half, half), half)
    span = pl.ds(pl.multiple_of(core * depth, depth), depth)
    rows = pl.ds(pl.multiple_of(core * tok, tok), tok)
    sib = p.sibling()
    slot_f = wall.at[chip, span, pl.ds(0, half)]
    slot_l = wall.at[chip, span, pl.ds(half, HD)]
    rem = [
        remote(wq_ref.at[:, theirs], slot_f, snd.at[0], rcv.at[0], sib),
        None,
        remote(x_ref, hid.at[rows], snd.at[2], rcv.at[2], sib),
        remote(aux_ref, aux.at[rows], snd.at[3], rcv.at[3], sib),
    ]
    own = [
        pltpu.make_async_copy(wq_ref.at[:, mine], slot_f, loc.at[0]),
        None,
        pltpu.make_async_copy(x_ref, hid.at[rows], loc.at[2]),
        pltpu.make_async_copy(aux_ref, aux.at[rows], loc.at[3]),
    ]

    @pl.when(core == 0)
    def _():
        remote(wv_ref, slot_l, snd.at[1], rcv.at[1], sib).start()
        pltpu.make_async_copy(wk_ref, slot_l, loc.at[1]).start()

    @pl.when(core == 1)
    def _():
        remote(wk_ref, slot_l, snd.at[1], rcv.at[1], sib).start()
        pltpu.make_async_copy(wv_ref, slot_l, loc.at[1]).start()

    rem[1] = remote(wk_ref, slot_l, snd.at[1], rcv.at[1], sib)
    own[1] = pltpu.make_async_copy(wk_ref, slot_l, loc.at[1])
    for k in (0, 2, 3):
        rem[k].start()
        own[k].start()
    return rem, own


def wait_inputs(rem, own, ks):
    for k in ks:
        own[k].wait()
        rem[k].wait_send()
        rem[k].wait_recv()


def turn(u, cosine, sine):
    return u * cosine + pltpu.roll(u, 64, 1) * sine


def angles(positions):
    half = HD // 2
    inverse = 500000.0 ** (-(jnp.arange(half, dtype=jnp.float32) * 2.0 / HD))
    angle = positions.astype(jnp.float32)[:, None] * inverse[None, :]
    cosine, sine = jnp.cos(angle), jnp.sin(angle)
    return jnp.concatenate([cosine, cosine, -sine, sine], axis=1)

def attend(q_ref, m_ref, l_ref, acc_ref, keys, values, visible=None):
    rows = q_ref.shape[0] // 2
    for h in range(2):
        at = pl.ds(h * rows, rows)
        score = lax.dot_general(q_ref[at], keys, (((1,), (1,)), ((), ())), preferred_element_type=jnp.float32)
        if visible is not None:
            score = jnp.where(visible, score, NEGATIVE)
        before = m_ref[at]
        peak = jnp.maximum(before, jnp.max(score, axis=1, keepdims=True))
        fade = jnp.exp2((before - peak) * SCALE)
        weight = jnp.exp2((score - peak) * SCALE)
        m_ref[at] = peak
        l_ref[at] = l_ref[at] * fade + jnp.sum(weight, axis=1, keepdims=True)
        acc_ref[at] = acc_ref[at] * fade + jnp.dot(
            weight.astype(jnp.bfloat16), values, preferred_element_type=jnp.float32)


def planned(step):
    at = jnp.int32(-1)
    for when, what in O_PLAN:
        at = jnp.where(step == when, what, at)
    return at


def block_kernel(x_ref, wq_ref, wk_ref, wv_ref, wo_ref, aux_ref, gain_ref, out_ref,
                 hid, aux, wall, full, kv, oall, qs, m_ref, l_ref, acc, att,
                 part, xin, zout, zin, fin, tin, loc, snd, rcv, sib_s, sib_r, att_sem, x_s, x_r, z_s, z_r, t_s, t_r, *gsems):
    p = Place()
    core, chip = p.core, p.chip
    tok = x_ref.shape[0]
    sib = p.sibling()
    entry(p)
    rem, own = load_inputs(p, x_ref, wq_ref, wk_ref, wv_ref, aux_ref, hid, aux, wall, loc, snd, rcv)
    o_own = pltpu.make_async_copy(wo_ref, oall.at[chip], loc.at[4])
    o_own.start()
    n = len(gsems) // 3
    g_w = Gather(p, wall, 96, gsems[:n])
    g_o = Gather(p, oall, 48, gsems[n:2 * n])
    g_kv = Gather(p, kv.at[core], 192, gsems[2 * n:])
    wait_inputs(rem, own, (0, 1))
    g_w.begin()
    full[...] = jnp.zeros_like(full)

    def project(t, _):
        g_w.round(t)
        @pl.when(t == O_BEGIN)
        def _():
            o_own.wait()
            g_o.begin()

        g_o.round(planned(t))
        d = t - USE_AT

        def use(g, _):
            @pl.when((g >= 0) & (g < ROWS))
            def _():
                row = g_w.row(g)
                g_w.line_arrived(row)
                depth = LINE * 128
                left = hid[:, pl.ds(pl.multiple_of(row * depth, depth), depth)]
                at = pl.ds(pl.multiple_of(row * LINE, LINE), LINE)
                full[...] += jnp.dot(left, wall[at].reshape(depth, wall.shape[2]), preferred_element_type=jnp.float32)
            return 0

        @pl.when(d == 0)
        def _():
            wait_inputs(rem, own, (2, 3))

        @pl.when(d >= 0)
        def _():
            lax.fori_loop(2 * d - 1, 2 * d + 1, use, 0)
        return 0

    lax.fori_loop(0, STEPS, project, 0)

    cosine, sine = aux[:, 0:HD], aux[:, HD:2 * HD]
    last = full[:, 2 * HD:]
    kv[core, chip] = jnp.where(core == 0, turn(last, cosine, sine), last).astype(jnp.bfloat16)
    def relay(slots, sem, kind):
        ref = kv.at[kind, slots]
        return remote(ref, ref, sib_s.at[0], sib_r.at[sem], sib)

    relay(pl.ds(chip, 1), ROWS, core).start()
    g_kv.begin()
    for h in range(2):
        qs[pl.ds(2 * tok * h, 2 * tok)] = turn(full[:, h * HD:(h + 1) * HD], cosine, sine).astype(jnp.bfloat16)
    m_ref[...] = jnp.full_like(m_ref, NEGATIVE)
    l_ref[...] = jnp.zeros_like(l_ref)
    acc[...] = jnp.zeros_like(acc)

    def block(kind, start, count):
        return kv[kind, pl.ds(start, count)].reshape(count * 2 * tok, HD)

    def look(t, _):
        g_kv.round(t)
        g_o.round(planned(t + STEPS))
        d = t - USE_AT

        @pl.when(t == 0)
        def _():
            relay(pl.ds(chip, 1), ROWS, 1 - core).wait_recv()
            vis = aux[:, 2 * HD:3 * HD]
            visible = jnp.concatenate([
                jnp.concatenate([vis[:tok], jnp.zeros_like(vis[:tok])], axis=1),
                jnp.concatenate([jnp.ones_like(vis[tok:]), vis[tok:]], axis=1)], axis=0) > 0.5
            attend(qs, m_ref, l_ref, acc, block(0, chip, 1), block(1, chip, 1), visible)

        @pl.when(d == 0)
        def _():
            g_kv.line_arrived(p.y)
            for i in range(1, LINE):
                relay(pl.ds(p.y * LINE + p.order(i), 1), p.y, core).start()
            relay(pl.ds(0, LINE - 1), p.y, 1 - core).wait_recv()

            def one(z, _):
                slot = p.y * LINE + z
                attend(qs, m_ref, l_ref, acc, block(0, slot, 1), block(1, slot, 1))
                return 0
            lax.fori_loop(0, p.z, one, 0)

        def forward(g, _):
            @pl.when((g >= 1) & (g < ROWS))
            def _():
                row = g_kv.row(g)
                g_kv.line_arrived(row)
                relay(pl.ds(pl.multiple_of(row * LINE, LINE), LINE), row, core).start()
            return 0

        def use(g, _):
            @pl.when((g >= 1) & (g < ROWS))
            def _():
                row = g_kv.row(g)
                start = pl.multiple_of(row * LINE, LINE)
                relay(pl.ds(start, LINE), row, 1 - core).wait_recv()
                pl.when(row < p.y)(lambda: attend(qs, m_ref, l_ref, acc, block(0, start, LINE), block(1, start, LINE)))
            return 0

        @pl.when(d >= 1)
        def _():
            lax.fori_loop(2 * d - 1, 2 * d + 1, forward, 0)
            lax.fori_loop(2 * d - 1, 2 * d + 1, use, 0)
        return 0

    lax.fori_loop(0, STEPS, look, 0)

    done = (acc[...] / l_ref[...]).astype(jnp.bfloat16)
    share = tok // 8
    for h in range(2):
        for xt in range(4):
            for zt in range(2):
                for c in range(2):
                    src = h * 2 * tok + c * tok + (zt * 4 + xt) * share
                    dst = (xt * 4 + zt * 2 + c) * share
                    att[core, dst:dst + share, h * HD:(h + 1) * HD] = done[src:src + share]
    swap = remote(att.at[core], att.at[core], att_sem.at[0], att_sem.at[1], sib)
    swap.start()
    swap.wait()

    span = LINE * 64
    piece = 4 * share
    wide_chunk = 2 * span

    def x_copies(c):
        cols = pl.ds(pl.multiple_of(c * wide_chunk, wide_chunk), wide_chunk)
        return [remote(part.at[(p.x + step) % 4, :, cols], xin.at[k, :, cols], x_s.at[0], x_r.at[k, c], p.across(step))
                for k, step in enumerate((2, 1, 3))]

    def keep(which):
        return pl.ds(pl.multiple_of(which * share, share), share)

    def z_copy(cols, to):
        return remote(zout.at[keep(to), cols], zin.at[core, :, cols], z_s.at[0], z_r.at[core], p.far(to))

    def t_copy(cols):
        return remote(fin.at[1 - core, :, cols], tin.at[:, cols], t_s.at[0], t_r.at[0], sib)

    def produce(c):
        for half in range(2):
            g = 2 * c + half
            r = g_o.row(g)
            at = pl.ds(pl.multiple_of(r * LINE, LINE), LINE)
            g_o.line_arrived(r)
            left = jnp.concatenate([att[0], att[1]], axis=1)
            prod = lax.dot_general(left, oall[at].reshape(span, oall.shape[2]), (((1,), (1,)), ((), ())),
                                   preferred_element_type=jnp.float32)
            part[:, :, pl.ds(pl.multiple_of(g * span, span), span)] = prod.astype(jnp.bfloat16).reshape(4, piece, span)
        for cp in x_copies(c):
            cp.start()

    def merge(c):
        cols = pl.ds(pl.multiple_of(c * wide_chunk, wide_chunk), wide_chunk)
        for cp in x_copies(c):
            cp.wait_recv()
        half = piece // 2

        def summed(z):
            at = pl.ds(pl.multiple_of(z * half, half), half)
            f = lambda v: v.astype(jnp.float32)
            return f(part[p.x, at, cols]) + f(xin[0, at, cols]) + f(xin[1, at, cols]) + f(xin[2, at, cols])

        zout[:, cols] = summed(1 - p.zh).astype(jnp.bfloat16)
        z_copy(cols, core).start()
        z_copy(cols, 1 - core).start()
        fin[:, :, cols] = summed(p.zh).reshape(2, share, wide_chunk)
        t_copy(cols).start()

    chunks = ROWS // 2

    def flow(s, _):
        pl.when(s < chunks)(lambda: produce(s))
        g_o.round(planned(s + 2 * STEPS))
        pl.when(s >= MERGE_AT)(lambda: merge(s - MERGE_AT))
        return 0

    lax.fori_loop(0, chunks + MERGE_AT, flow, 0)
    remote(tin, tin, t_s.at[0], t_r.at[0], sib).wait_recv()
    for k in range(2):
        remote(zin.at[k], zin.at[k], z_s.at[0], z_r.at[k], sib).wait_recv()
    mine = fin[core] + zin[core].astype(jnp.float32)
    theirs = tin[...] + zin[1 - core].astype(jnp.float32)
    even = jnp.where(core == 0, mine, theirs)
    odd = jnp.where(core == 0, theirs, mine)
    low = lax.broadcasted_iota(jnp.int32, (share, HD), 1) < HD // 2
    at = pl.ds(pl.multiple_of(core * tok + p.head * share, share), share)
    square = jnp.zeros((share, 1), jnp.float32)
    tiles = []
    for g in range(ROWS):
        for m in range(2):
            cut = g * span + m * HD
            a, b = even[:, cut:cut + HD], odd[:, cut:cut + HD]
            pair = (jnp.where(low, a, pltpu.roll(b, 64, 1)), jnp.where(low, pltpu.roll(a, 64, 1), b))
            for k in range(2):
                cols = pl.ds(pl.multiple_of(g_o.row(g) * 2 * span + (2 * m + k) * HD, HD), HD)
                value = pair[k] + hid[at, cols].astype(jnp.float32)
                square += jnp.sum(value * value, axis=1, keepdims=True)
                tiles.append((cols, value))
    norm = lax.rsqrt(square * (1.0 / (CHIPS * HD)) + 1e-05)
    for cols, value in tiles:
        out_ref[:, cols] = (value * norm * gain_ref[:, cols]).astype(jnp.bfloat16)

    g_w.drain()
    g_o.drain()
    g_kv.drain()

    remote(xin, xin, x_s.at[0], x_r.at[0, 0], p.across(1)).wait_send()

    remote(zout, zout, z_s.at[0], z_r.at[0], sib).wait_send()
    remote(tin, tin, t_s.at[0], t_r.at[0], sib).wait_send()
    relay(pl.ds(0, CHIPS), 0, core).wait_send()


def whole(x, wq, wk, wv, wo, aux, gain):
    tok = x.shape[0]
    width = x.shape[1]
    dma = pltpu.SemaphoreType.DMA
    anyspec = pl.BlockSpec(memory_space=pl.ANY)
    vm = pl.BlockSpec(memory_space=pltpu.VMEM)
    bf, f32 = jnp.bfloat16, jnp.float32
    share = tok // 8
    half = width // 2
    return pl.pallas_call(
        block_kernel,
        out_shape=jax.ShapeDtypeStruct((share, width), bf),
        in_specs=[anyspec] * 6 + [vm],
        out_specs=vm,
        scratch_shapes=[
            pltpu.VMEM((2 * tok, width), bf),
            pltpu.VMEM((2 * tok, aux.shape[1]), f32),
            pltpu.VMEM((CHIPS, 128, 384), bf),
            pltpu.VMEM((2 * tok, 384), f32),
            pltpu.VMEM((2, CHIPS, 2 * tok, HD), bf),
            pltpu.VMEM((CHIPS, 64, 512), bf),
            pltpu.VMEM((4 * tok, HD), bf),
            pltpu.VMEM((4 * tok, 1), f32),
            pltpu.VMEM((4 * tok, 1), f32),
            pltpu.VMEM((4 * tok, HD), f32),
            pltpu.VMEM((2, 2 * tok, 256), bf),
            pltpu.VMEM((4, 4 * share, half), bf),
            pltpu.VMEM((3, 4 * share, half), bf),
            pltpu.VMEM((2 * share, half), bf),
            pltpu.VMEM((2, share, half), bf),
            pltpu.VMEM((2, share, half), f32),
            pltpu.VMEM((share, half), f32),
            dma((5,)), dma((4,)), dma((4,)),
            dma((1,)), dma((ROWS + 1,)), dma((2,)),
            dma((1,)), dma((3, 4)), dma((1,)), dma((2,)), dma((1,)), dma((1,)),
        ] + Gather.scratch() * 3,
        compiler_params=pltpu.CompilerParams(collective_id=0, has_side_effects=True, vmem_limit_bytes=56 << 20),
        name="block",
    )(x, wq, wk, wv, wo, aux, gain)


def on_device(hidden_in, positions, w_query, w_key, w_value, w_out, norm_gain):
    visible = (positions[None, :] <= positions[:, None]).astype(jnp.float32)
    aux = jnp.concatenate([angles(positions), visible], axis=1)
    return whole(hidden_in, w_query, w_key, w_value, w_out.T, aux, norm_gain.reshape(1, -1))


def solution(mesh):
    return jax.shard_map(
        on_device,
        mesh=mesh,
        in_specs=(P("ctx", None), P("ctx"), P("ctx", "head"), P("ctx", "head"), P("ctx", "head"), P("head", "ctx"), P()),
        out_specs=P(("ctx", "head"), None),
        check_vma=False,
    )
```

```python
import jax
import jax.numpy as jnp
from jax import lax
from jax.experimental import pallas as pl
from jax.experimental.pallas import tpu as pltpu
from jax.sharding import PartitionSpec as P
import numpy as np

MESH = pl.DeviceIdType.MESH
HD = 128
ROWS = 8
LINE = 4
CHIPS = ROWS * LINE
ROUNDS = ROWS // 2 + 2
USE_AT = 2
STEPS = ROUNDS + USE_AT - 1
O_BEGIN = 0
O_PLAN = ((5, 1), (12, 2), (13, 3), (15, 4), (17, 5))
MERGE_AT = 3
NEGATIVE = -1e30
SCALE = 1.4426950408889634 / HD ** 0.5


class Place:
    def __init__(self):
        ctx = lax.axis_index("ctx")
        head = lax.axis_index("head")
        self.core = ctx % 2
        self.z = (ctx // 2) % LINE
        self.y = ctx // (2 * LINE)
        self.x = head % 4
        self.zh = head // 4
        self.chip = ctx // 2
        self.ctx = ctx
        self.head = head

    def at(self, y, z, core):
        return ((y * LINE + z) * 2 + core, self.head)

    def sibling(self):
        return (self.chip * 2 + 1 - self.core, self.head)

    def up(self):
        return self.at((self.y + 1) % ROWS, self.z, self.core)

    def down(self):
        return self.at((self.y + ROWS - 1) % ROWS, self.z, self.core)

    def across(self, steps):
        return (self.ctx, self.zh * 4 + (self.x + 4 + steps) % 4)

    def far(self, core):
        return (self.chip * 2 + core, (1 - self.zh) * 4 + self.x)

    def order(self, i):
        z = self.z
        if i == 0:
            return z
        a = (1, 0, 3, 2)
        b = (2, 2, 1, 1)
        c = (3, 3, 0, 0)
        t = (a, b, c)[i - 1]
        return jnp.where(z == 0, t[0], jnp.where(z == 1, t[1], jnp.where(z == 2, t[2], t[3])))


class Gather:
    def __init__(self, place, buf, cut, sems):
        self.p = place
        self.buf, self.cut = buf, cut
        self.rf, self.ly, self.lz, self.out = sems

    @staticmethod
    def scratch():
        dma = pltpu.SemaphoreType.DMA
        return [dma((CHIPS,)), dma((ROWS,)), dma((ROWS,)), dma((1,))]

    def row(self, g):
        d = (g + 1) // 2
        up = jnp.logical_and(g % 2 == 1, jnp.logical_or(g < 7, self.p.core == 0))
        return jnp.where(up, self.p.y + ROWS - d, self.p.y + d) % ROWS

    def first(self, slot):
        return self.buf.at[slot, pl.ds(0, self.cut)]

    def last(self, slot):
        return self.buf.at[slot, pl.ds(self.cut, self.buf.shape[1] - self.cut)]

    def copy(self, ref, sem, device):
        return remote(ref, ref, self.out.at[0], sem, device)

    def onward(self, g):
        core = self.p.core
        return ((g == 1) | (g == 3) | ((g == 5) & (core == 0)),
                (g == 2) | (g == 4) | ((g == 6) & (core == 1)))

    def along(self, make, g):
        up, down = self.onward(g)

        @pl.when(up)
        def _():
            make(self.p.up()).start()

        @pl.when(down)
        def _():
            make(self.p.down()).start()

    def line(self, make):
        for i in range(1, LINE):
            make(self.p.at(self.p.y, self.p.order(i), self.p.core)).start()

    def begin(self):
        p = self.p
        slot = p.chip
        self.line(lambda dev: self.copy(self.first(slot), self.rf.at[slot], dev))
        for dev in (p.up(), p.down()):
            self.copy(self.last(slot), self.ly.at[p.y], dev).start()
            self.copy(self.first(slot), self.rf.at[slot], dev).start()
        self.line(lambda dev: self.copy(self.last(slot), self.lz.at[p.y], dev))

    def near(self, g):
        row = self.row(g)
        slot = row * LINE + self.p.z
        here = self.copy(self.last(slot), self.ly.at[row], self.p.up())
        here.wait_recv()
        self.along(lambda dev: self.copy(self.last(slot), self.ly.at[row], dev), g)
        self.line(lambda dev: self.copy(self.last(slot), self.lz.at[row], dev))
        self.pass_on(g, slot)

    def pass_on(self, g, slot):
        make = lambda dev: self.copy(self.first(slot), self.rf.at[slot], dev)
        make(self.p.up()).wait_recv()
        self.along(make, g)

    def others(self, g):
        row = self.row(g)
        for i in range(1, LINE):
            self.pass_on(g, row * LINE + self.p.order(i))

    def line_arrived(self, row):
        three = self.buf.at[pl.ds(0, LINE - 1), pl.ds(self.cut, self.buf.shape[1] - self.cut)]
        self.copy(three, self.lz.at[row], self.p.up()).wait_recv()

    def round(self, t):
        for g in (2 * t - 1, 2 * t):
            pl.when((g >= 1) & (g < ROWS))(lambda g=g: self.near(g))

        @pl.when(t == 1)
        def _():
            for i in range(1, LINE):
                slot = self.p.y * LINE + self.p.order(i)
                make = lambda dev: self.copy(self.first(slot), self.rf.at[slot], dev)
                make(self.p.up()).wait_recv()
                make(self.p.up()).start()
                make(self.p.down()).start()

        for g in (2 * t - 3, 2 * t - 2):
            pl.when((g >= 1) & (g < ROWS))(lambda g=g: self.others(g))

    def drain(self):
        sent = self.buf.at[pl.ds(0, CHIPS - 1)]
        self.copy(sent, self.ly.at[0], self.p.up()).wait_send()


def remote(src, dst, send, recv, device):
    return pltpu.make_async_remote_copy(
        src_ref=src, dst_ref=dst, send_sem=send, recv_sem=recv, device_id=device, device_id_type=MESH)


def entry(p):
    bar = pltpu.get_barrier_semaphore()
    devices = [p.far(p.core), p.far(1 - p.core), p.across(2)] + [p.at(p.y, p.order(i), p.core) for i in range(LINE - 1, 0, -1)]
    devices += [p.across(1), p.across(-1), p.up(), p.down(), p.sibling()]
    for d in devices:
        pl.semaphore_signal(bar, inc=1, device_id=d, device_id_type=MESH)
    pl.semaphore_wait(bar, len(devices))


class Inputs:
    def __init__(self, p, x_ref, wq_ref, wk_ref, wv_ref, pos_ref, hid, pos, wall, loc, snd, rcv):
        core = p.core
        tok = x_ref.shape[0]
        depth = wq_ref.shape[0]
        half = wq_ref.shape[1] // 2
        columns = lambda c: pl.ds(pl.multiple_of(c * half, half), half)
        span = pl.ds(pl.multiple_of(core * depth, depth), depth)
        rows = pl.ds(pl.multiple_of(core * tok, tok), tok)
        slot_q = wall.at[p.chip, span, pl.ds(0, half)]
        slot_l = wall.at[p.chip, span, pl.ds(half, HD)]
        self.core = core
        self.narrow = (wk_ref, wv_ref)
        self.local = lambda ref, dst, k: pltpu.make_async_copy(ref, dst, loc.at[k])
        self.cross = lambda ref, dst, k: remote(ref, dst, snd.at[k], rcv.at[k], p.sibling())
        self.slot_l = slot_l
        pairs = ((wq_ref.at[:, columns(core)], wq_ref.at[:, columns(1 - core)], slot_q), None,
                 (x_ref, x_ref, hid.at[rows]), (pos_ref, pos_ref, pos.at[core]))
        self.own = [self.local(q[0], q[2], k) if q else self.local(wk_ref, slot_l, 1) for k, q in enumerate(pairs)]
        self.sent = [self.cross(q[1], q[2], k) if q else self.cross(wk_ref, slot_l, 1) for k, q in enumerate(pairs)]

    def start(self, far):
        make = self.cross if far else self.local
        for c in range(2):
            kept = self.narrow[1 - c if far else c]
            pl.when(self.core == c)(lambda kept=kept: make(kept, self.slot_l, 1).start())
        for k in (0, 3, 2):
            (self.sent if far else self.own)[k].start()

    def wait(self, *ks):
        for k in ks:
            self.own[k].wait()
            self.sent[k].wait_send()
            self.sent[k].wait_recv()


def turn(u, cosine, sine):
    return u * cosine + pltpu.roll(u, 64, 1) * sine


def attend(q_ref, m_ref, l_ref, acc_ref, keys, values, visible=None):
    rows = q_ref.shape[0] // 2
    for h in range(2):
        at = pl.ds(h * rows, rows)
        score = lax.dot_general(q_ref[at], keys, (((1,), (1,)), ((), ())), preferred_element_type=jnp.float32)
        if visible is not None:
            score = jnp.where(visible, score, NEGATIVE)
        before = m_ref[at]
        peak = jnp.maximum(before, jnp.max(score, axis=1, keepdims=True))
        fade = jnp.exp2((before - peak) * SCALE)
        weight = jnp.exp2((score - peak) * SCALE)
        m_ref[at] = peak
        l_ref[at] = l_ref[at] * fade + jnp.sum(weight, axis=1, keepdims=True)
        acc_ref[at] = acc_ref[at] * fade + jnp.dot(
            weight.astype(jnp.bfloat16), values, preferred_element_type=jnp.float32)


def planned(step):
    at = jnp.int32(-1)
    for when, what in O_PLAN:
        at = jnp.where(step == when, what, at)
    return at


def block_kernel(x_ref, wq_ref, wk_ref, wv_ref, wo_ref, pos_ref, freq_ref, gain_ref, out_ref,
                 hid, pos, freq, gain, aux, seen, wall, full, kv, oall, qs, m_ref, l_ref, acc, att,
                 part, xin, zout, zin, fin, tin, loc, snd, rcv, sib_s, sib_r, att_sem, x_s, x_r, z_s, z_r, t_s, t_r, *gsems):
    p = Place()
    core, chip = p.core, p.chip
    tok = x_ref.shape[0]
    sib = p.sibling()
    given = Inputs(p, x_ref, wq_ref, wk_ref, wv_ref, pos_ref, hid, pos, wall, loc, snd, rcv)
    o_own = pltpu.make_async_copy(wo_ref, oall.at[chip], loc.at[4])
    f_own = pltpu.make_async_copy(freq_ref, freq, loc.at[5])
    n_own = pltpu.make_async_copy(gain_ref, gain, loc.at[6])
    given.start(False)
    for c in (f_own, o_own, n_own):
        c.start()
    entry(p)
    given.start(True)
    n = len(gsems) // 3
    g_w = Gather(p, wall, 96, gsems[:n])
    g_o = Gather(p, oall, 48, gsems[n:2 * n])
    g_kv = Gather(p, kv.at[core], 192, gsems[2 * n:])
    given.wait(0, 1)
    g_w.begin()
    full[...] = jnp.zeros_like(full)

    given.wait(3)
    f_own.wait()
    sign = jnp.where(lax.broadcasted_iota(jnp.int32, (1, HD), 1) < HD // 2, -1.0, 1.0)
    for c in range(2):
        at = pl.ds(c * tok, tok)
        column = jnp.transpose(jnp.broadcast_to(pos[c].astype(jnp.float32), (tok, tok)))
        angle = column * freq[...]
        aux[at, 0:HD] = jnp.cos(angle)
        aux[at, HD:2 * HD] = jnp.sin(angle) * sign
        for k in range(2):
            seen[at, k * tok:(k + 1) * tok] = (pos[k].astype(jnp.float32) <= column).astype(jnp.float32)

    def project(t, _):
        g_w.round(t)
        @pl.when(t == O_BEGIN)
        def _():
            o_own.wait()
            g_o.begin()

        g_o.round(planned(t))
        d = t - USE_AT

        def use(g, _):
            @pl.when((g >= 0) & (g < ROWS))
            def _():
                row = g_w.row(g)
                g_w.line_arrived(row)
                depth = LINE * 128
                left = hid[:, pl.ds(pl.multiple_of(row * depth, depth), depth)]
                at = pl.ds(pl.multiple_of(row * LINE, LINE), LINE)
                full[...] += jnp.dot(left, wall[at].reshape(depth, wall.shape[2]), preferred_element_type=jnp.float32)
            return 0

        @pl.when(d == 0)
        def _():
            given.wait(2)

        @pl.when(d >= 0)
        def _():
            lax.fori_loop(2 * d - 1, 2 * d + 1, use, 0)
        return 0

    lax.fori_loop(0, STEPS, project, 0)

    cosine, sine = aux[:, 0:HD], aux[:, HD:2 * HD]
    last = full[:, 2 * HD:]
    kv[core, chip] = jnp.where(core == 0, turn(last, cosine, sine), last).astype(jnp.bfloat16)
    def relay(slots, sem, kind):
        ref = kv.at[kind, slots]
        return remote(ref, ref, sib_s.at[0], sib_r.at[sem], sib)

    relay(pl.ds(chip, 1), ROWS, core).start()
    g_kv.begin()
    for h in range(2):
        qs[pl.ds(2 * tok * h, 2 * tok)] = turn(full[:, h * HD:(h + 1) * HD], cosine, sine).astype(jnp.bfloat16)
    m_ref[...] = jnp.full_like(m_ref, NEGATIVE)
    l_ref[...] = jnp.zeros_like(l_ref)
    acc[...] = jnp.zeros_like(acc)

    def block(kind, start, count):
        return kv[kind, pl.ds(start, count)].reshape(count * 2 * tok, HD)

    def look(t, _):
        g_kv.round(t)
        g_o.round(planned(t + STEPS))
        d = t - USE_AT

        @pl.when(t == 0)
        def _():
            relay(pl.ds(chip, 1), ROWS, 1 - core).wait_recv()
            attend(qs, m_ref, l_ref, acc, block(0, chip, 1), block(1, chip, 1), seen[...] > 0.5)

        @pl.when(d == 0)
        def _():
            g_kv.line_arrived(p.y)
            for i in range(1, LINE):
                relay(pl.ds(p.y * LINE + p.order(i), 1), p.y, core).start()
            relay(pl.ds(0, LINE - 1), p.y, 1 - core).wait_recv()

            def one(z, _):
                slot = p.y * LINE + z
                attend(qs, m_ref, l_ref, acc, block(0, slot, 1), block(1, slot, 1))
                return 0
            lax.fori_loop(0, p.z, one, 0)

        def forward(g, _):
            @pl.when((g >= 1) & (g < ROWS))
            def _():
                row = g_kv.row(g)
                g_kv.line_arrived(row)
                relay(pl.ds(pl.multiple_of(row * LINE, LINE), LINE), row, core).start()
            return 0

        def use(g, _):
            @pl.when((g >= 1) & (g < ROWS))
            def _():
                row = g_kv.row(g)
                start = pl.multiple_of(row * LINE, LINE)
                relay(pl.ds(start, LINE), row, 1 - core).wait_recv()
                pl.when(row < p.y)(lambda: attend(qs, m_ref, l_ref, acc, block(0, start, LINE), block(1, start, LINE)))
            return 0

        @pl.when(d >= 1)
        def _():
            lax.fori_loop(2 * d - 1, 2 * d + 1, forward, 0)
            lax.fori_loop(2 * d - 1, 2 * d + 1, use, 0)
        return 0

    lax.fori_loop(0, STEPS, look, 0)

    done = (acc[...] / l_ref[...]).astype(jnp.bfloat16)
    share = tok // 8
    for h in range(2):
        for xt in range(4):
            for zt in range(2):
                for c in range(2):
                    src = h * 2 * tok + c * tok + (zt * 4 + xt) * share
                    dst = (xt * 4 + zt * 2 + c) * share
                    att[core, dst:dst + share, h * HD:(h + 1) * HD] = done[src:src + share]
    swap = remote(att.at[core], att.at[core], att_sem.at[0], att_sem.at[1], sib)
    swap.start()
    swap.wait()

    span = LINE * 64
    piece = 4 * share
    wide_chunk = span

    def x_copies(c):
        cols = pl.ds(pl.multiple_of(c * wide_chunk, wide_chunk), wide_chunk)
        return [remote(part.at[(p.x + step) % 4, :, cols], xin.at[k, :, cols], x_s.at[0], x_r.at[k, c], p.across(step))
                for k, step in enumerate((2, 1, 3))]

    def keep(which):
        return pl.ds(pl.multiple_of(which * share, share), share)

    def z_copy(cols, to):
        return remote(zout.at[keep(to), cols], zin.at[core, :, cols], z_s.at[0], z_r.at[core], p.far(to))

    def t_copy(cols):
        return remote(fin.at[1 - core, :, cols], tin.at[:, cols], t_s.at[0], t_r.at[0], sib)

    def produce(g):
        r = g_o.row(g)
        at = pl.ds(pl.multiple_of(r * LINE, LINE), LINE)
        g_o.line_arrived(r)
        left = jnp.concatenate([att[0], att[1]], axis=1)
        prod = lax.dot_general(left, oall[at].reshape(span, oall.shape[2]), (((1,), (1,)), ((), ())),
                               preferred_element_type=jnp.float32)
        part[:, :, pl.ds(pl.multiple_of(g * span, span), span)] = prod.astype(jnp.bfloat16).reshape(4, piece, span)
        for cp in x_copies(g):
            cp.start()

    def merge(c):
        cols = pl.ds(pl.multiple_of(c * wide_chunk, wide_chunk), wide_chunk)
        for cp in x_copies(c):
            cp.wait_recv()
        half = piece // 2

        def summed(z):
            at = pl.ds(pl.multiple_of(z * half, half), half)
            f = lambda v: v.astype(jnp.float32)
            return f(part[p.x, at, cols]) + f(xin[0, at, cols]) + f(xin[1, at, cols]) + f(xin[2, at, cols])

        zout[:, cols] = summed(1 - p.zh).astype(jnp.bfloat16)
        z_copy(cols, core).start()
        z_copy(cols, 1 - core).start()
        fin[:, :, cols] = summed(p.zh).reshape(2, share, wide_chunk)
        t_copy(cols).start()

    chunks = ROWS

    def flow(s, _):
        pl.when(s < chunks)(lambda: produce(s))
        g_o.round(planned(s + 2 * STEPS))
        pl.when(s >= MERGE_AT)(lambda: merge(s - MERGE_AT))
        return 0

    lax.fori_loop(0, chunks + MERGE_AT, flow, 0)
    remote(tin, tin, t_s.at[0], t_r.at[0], sib).wait_recv()
    for k in range(2):
        remote(zin.at[k], zin.at[k], z_s.at[0], z_r.at[k], sib).wait_recv()
    mine = fin[core] + zin[core].astype(jnp.float32)
    theirs = tin[...] + zin[1 - core].astype(jnp.float32)
    even = jnp.where(core == 0, mine, theirs)
    odd = jnp.where(core == 0, theirs, mine)
    low = lax.broadcasted_iota(jnp.int32, (share, HD), 1) < HD // 2
    at = pl.ds(pl.multiple_of(core * tok + p.head * share, share), share)
    square = jnp.zeros((share, 1), jnp.float32)
    tiles = []
    for g in range(ROWS):
        for m in range(2):
            cut = g * span + m * HD
            a, b = even[:, cut:cut + HD], odd[:, cut:cut + HD]
            pair = (jnp.where(low, a, pltpu.roll(b, 64, 1)), jnp.where(low, pltpu.roll(a, 64, 1), b))
            for k in range(2):
                cols = pl.ds(pl.multiple_of(g_o.row(g) * 2 * span + (2 * m + k) * HD, HD), HD)
                value = pair[k] + hid[at, cols].astype(jnp.float32)
                square += jnp.sum(value * value, axis=1, keepdims=True)
                tiles.append((cols, value))
    n_own.wait()
    norm = lax.rsqrt(square * (1.0 / (CHIPS * HD)) + 1e-05)
    for cols, value in tiles:
        out_ref[:, cols] = (value * norm * gain[:, cols]).astype(jnp.bfloat16)

    g_w.drain()
    g_o.drain()
    g_kv.drain()

    remote(xin, xin, x_s.at[0], x_r.at[0, 0], p.across(1)).wait_send()

    remote(zout, zout, z_s.at[0], z_r.at[0], sib).wait_send()
    remote(tin, tin, t_s.at[0], t_r.at[0], sib).wait_send()
    relay(pl.ds(0, CHIPS), 0, core).wait_send()


def whole(x, wq, wk, wv, wo, pos, freq, gain):
    tok = x.shape[0]
    width = x.shape[1]
    dma = pltpu.SemaphoreType.DMA
    anyspec = pl.BlockSpec(memory_space=pl.ANY)
    vm = pl.BlockSpec(memory_space=pltpu.VMEM)
    bf, f32 = jnp.bfloat16, jnp.float32
    share = tok // 8
    half = width // 2
    return pl.pallas_call(
        block_kernel,
        out_shape=jax.ShapeDtypeStruct((share, width), bf),
        in_specs=[anyspec] * 8,
        out_specs=vm,
        scratch_shapes=[
            pltpu.VMEM((2 * tok, width), bf),
            pltpu.VMEM((2, 1, tok), jnp.int32),
            pltpu.VMEM((1, HD), f32),
            pltpu.VMEM((1, width), f32),
            pltpu.VMEM((2 * tok, 2 * HD), f32),
            pltpu.VMEM((2 * tok, 2 * tok), f32),
            pltpu.VMEM((CHIPS, 128, 384), bf),
            pltpu.VMEM((2 * tok, 384), f32),
            pltpu.VMEM((2, CHIPS, 2 * tok, HD), bf),
            pltpu.VMEM((CHIPS, 64, 512), bf),
            pltpu.VMEM((4 * tok, HD), bf),
            pltpu.VMEM((4 * tok, 1), f32),
            pltpu.VMEM((4 * tok, 1), f32),
            pltpu.VMEM((4 * tok, HD), f32),
            pltpu.VMEM((2, 2 * tok, 256), bf),
            pltpu.VMEM((4, 4 * share, half), bf),
            pltpu.VMEM((3, 4 * share, half), bf),
            pltpu.VMEM((2 * share, half), bf),
            pltpu.VMEM((2, share, half), bf),
            pltpu.VMEM((2, share, half), f32),
            pltpu.VMEM((share, half), f32),
            dma((7,)), dma((4,)), dma((4,)),
            dma((1,)), dma((ROWS + 1,)), dma((2,)),
            dma((1,)), dma((3, ROWS)), dma((1,)), dma((2,)), dma((1,)), dma((1,)),
        ] + Gather.scratch() * 3,
        compiler_params=pltpu.CompilerParams(collective_id=0, has_side_effects=True, vmem_limit_bytes=56 << 20),
        name="block",
    )(x, wq, wk, wv, wo, pos, freq, gain)


def on_device(hidden_in, positions, w_query, w_key, w_value, w_out, norm_gain):
    half = np.arange(HD // 2, dtype=np.float64)
    freq = jnp.asarray(np.tile(500000.0 ** (-2.0 * half / HD), 2).astype(np.float32).reshape(1, HD))
    return whole(hidden_in, w_query, w_key, w_value, w_out.T, positions.reshape(1, -1), freq, norm_gain.reshape(1, -1))


def solution(mesh):
    return jax.shard_map(
        on_device,
        mesh=mesh,
        in_specs=(P("ctx", None), P("ctx"), P("ctx", "head"), P("ctx", "head"), P("ctx", "head"), P("head", "ctx"), P()),
        out_specs=P(("ctx", "head"), None),
        check_vma=False,
    )
```

```python
import jax
import jax.numpy as jnp
from jax import lax
from jax.experimental import pallas as pl
from jax.experimental.pallas import tpu as pltpu
from jax.sharding import PartitionSpec as P
import numpy as np

MESH = pl.DeviceIdType.MESH
HD = 128
ROWS = 8
LINE = 4
CHIPS = ROWS * LINE
ROUNDS = ROWS // 2 + 2
USE_AT = 2
STEPS = ROUNDS + USE_AT - 1
O_BEGIN = 0
O_PLAN = ((4, 1), (12, 2), (13, 3), (14, 4), (16, 5))
MERGE_AT = 3
NEGATIVE = -1e30
SCALE = 1.4426950408889634 / HD ** 0.5


class Place:
    def __init__(self):
        ctx = lax.axis_index("ctx")
        head = lax.axis_index("head")
        self.core = ctx % 2
        self.z = (ctx // 2) % LINE
        self.y = ctx // (2 * LINE)
        self.x = head % 4
        self.zh = head // 4
        self.chip = ctx // 2
        self.ctx = ctx
        self.head = head

    def at(self, y, z, core):
        return ((y * LINE + z) * 2 + core, self.head)

    def sibling(self):
        return (self.chip * 2 + 1 - self.core, self.head)

    def up(self):
        return self.at((self.y + 1) % ROWS, self.z, self.core)

    def down(self):
        return self.at((self.y + ROWS - 1) % ROWS, self.z, self.core)

    def across(self, steps):
        return (self.ctx, self.zh * 4 + (self.x + 4 + steps) % 4)

    def far(self, core):
        return (self.chip * 2 + core, (1 - self.zh) * 4 + self.x)

    def order(self, i):
        z = self.z
        if i == 0:
            return z
        a = (1, 0, 3, 2)
        b = (2, 2, 1, 1)
        c = (3, 3, 0, 0)
        t = (a, b, c)[i - 1]
        return jnp.where(z == 0, t[0], jnp.where(z == 1, t[1], jnp.where(z == 2, t[2], t[3])))


class Gather:
    def __init__(self, place, buf, cut, sems):
        self.p = place
        self.buf, self.cut = buf, cut
        self.rf, self.ly, self.lz, self.out = sems

    @staticmethod
    def scratch():
        dma = pltpu.SemaphoreType.DMA
        return [dma((CHIPS,)), dma((ROWS,)), dma((ROWS,)), dma((1,))]

    def row(self, g):
        d = (g + 1) // 2
        up = jnp.logical_and(g % 2 == 1, jnp.logical_or(g < 7, self.p.core == 0))
        return jnp.where(up, self.p.y + ROWS - d, self.p.y + d) % ROWS

    def first(self, slot):
        return self.buf.at[slot, pl.ds(0, self.cut)]

    def last(self, slot):
        return self.buf.at[slot, pl.ds(self.cut, self.buf.shape[1] - self.cut)]

    def copy(self, ref, sem, device):
        return remote(ref, ref, self.out.at[0], sem, device)

    def onward(self, g):
        core = self.p.core
        return ((g == 1) | (g == 3) | ((g == 5) & (core == 0)),
                (g == 2) | (g == 4) | ((g == 6) & (core == 1)))

    def along(self, make, g):
        up, down = self.onward(g)

        @pl.when(up)
        def _():
            make(self.p.up()).start()

        @pl.when(down)
        def _():
            make(self.p.down()).start()

    def line(self, make):
        for i in range(1, LINE):
            make(self.p.at(self.p.y, self.p.order(i), self.p.core)).start()

    def begin(self):
        p = self.p
        slot = p.chip
        self.line(lambda dev: self.copy(self.first(slot), self.rf.at[slot], dev))
        for dev in (p.up(), p.down()):
            self.copy(self.last(slot), self.ly.at[p.y], dev).start()
            self.copy(self.first(slot), self.rf.at[slot], dev).start()
        self.line(lambda dev: self.copy(self.last(slot), self.lz.at[p.y], dev))

    def near(self, g):
        row = self.row(g)
        slot = row * LINE + self.p.z
        here = self.copy(self.last(slot), self.ly.at[row], self.p.up())
        here.wait_recv()
        self.along(lambda dev: self.copy(self.last(slot), self.ly.at[row], dev), g)
        self.line(lambda dev: self.copy(self.last(slot), self.lz.at[row], dev))
        self.pass_on(g, slot)

    def pass_on(self, g, slot):
        make = lambda dev: self.copy(self.first(slot), self.rf.at[slot], dev)
        make(self.p.up()).wait_recv()
        self.along(make, g)

    def others(self, g):
        row = self.row(g)
        for i in range(1, LINE):
            self.pass_on(g, row * LINE + self.p.order(i))

    def line_arrived(self, row):
        three = self.buf.at[pl.ds(0, LINE - 1), pl.ds(self.cut, self.buf.shape[1] - self.cut)]
        self.copy(three, self.lz.at[row], self.p.up()).wait_recv()

    def round(self, t):
        for g in (2 * t - 1, 2 * t):
            pl.when((g >= 1) & (g < ROWS))(lambda g=g: self.near(g))

        @pl.when(t == 1)
        def _():
            for i in range(1, LINE):
                slot = self.p.y * LINE + self.p.order(i)
                make = lambda dev: self.copy(self.first(slot), self.rf.at[slot], dev)
                make(self.p.up()).wait_recv()
                make(self.p.up()).start()
                make(self.p.down()).start()

        for g in (2 * t - 3, 2 * t - 2):
            pl.when((g >= 1) & (g < ROWS))(lambda g=g: self.others(g))

    def drain(self):
        sent = self.buf.at[pl.ds(0, CHIPS - 1)]
        self.copy(sent, self.ly.at[0], self.p.up()).wait_send()


def remote(src, dst, send, recv, device):
    return pltpu.make_async_remote_copy(
        src_ref=src, dst_ref=dst, send_sem=send, recv_sem=recv, device_id=device, device_id_type=MESH)


def entry(p):
    bar = pltpu.get_barrier_semaphore()
    devices = [p.far(p.core), p.far(1 - p.core), p.across(2)] + [p.at(p.y, p.order(i), p.core) for i in range(LINE - 1, 0, -1)]
    devices += [p.across(1), p.across(-1), p.up(), p.down(), p.sibling()]
    for d in devices:
        pl.semaphore_signal(bar, inc=1, device_id=d, device_id_type=MESH)
    pl.semaphore_wait(bar, len(devices))


class Inputs:
    def __init__(self, p, x_ref, wq_ref, wk_ref, wv_ref, pos_ref, hid, pos, wall, loc, snd, rcv):
        core = p.core
        tok = x_ref.shape[0]
        depth = wq_ref.shape[0]
        half = wq_ref.shape[1] // 2
        columns = lambda c: pl.ds(pl.multiple_of(c * half, half), half)
        span = pl.ds(pl.multiple_of(core * depth, depth), depth)
        rows = pl.ds(pl.multiple_of(core * tok, tok), tok)
        slot_q = wall.at[p.chip, span, pl.ds(0, half)]
        slot_l = wall.at[p.chip, span, pl.ds(half, HD)]
        self.core = core
        self.narrow = (wk_ref, wv_ref)
        self.local = lambda ref, dst, k: pltpu.make_async_copy(ref, dst, loc.at[k])
        self.cross = lambda ref, dst, k: remote(ref, dst, snd.at[k], rcv.at[k], p.sibling())
        self.slot_l = slot_l
        pairs = ((wq_ref.at[:, columns(core)], wq_ref.at[:, columns(1 - core)], slot_q), None,
                 (x_ref, x_ref, hid.at[rows]), (pos_ref, pos_ref, pos.at[core]))
        self.own = [self.local(q[0], q[2], k) if q else self.local(wk_ref, slot_l, 1) for k, q in enumerate(pairs)]
        self.sent = [self.cross(q[1], q[2], k) if q else self.cross(wk_ref, slot_l, 1) for k, q in enumerate(pairs)]

    def start(self, far):
        make = self.cross if far else self.local
        for c in range(2):
            kept = self.narrow[1 - c if far else c]
            pl.when(self.core == c)(lambda kept=kept: make(kept, self.slot_l, 1).start())
        for k in (0, 3, 2):
            (self.sent if far else self.own)[k].start()

    def wait(self, *ks):
        for k in ks:
            self.own[k].wait()
            self.sent[k].wait_send()
            self.sent[k].wait_recv()


def turn(u, cosine, sine):
    return u * cosine + pltpu.roll(u, 64, 1) * sine


def attend(q_ref, m_ref, l_ref, acc_ref, keys, values, visible=None):
    rows = q_ref.shape[0] // 2
    for h in range(2):
        at = pl.ds(h * rows, rows)
        score = lax.dot_general(q_ref[at], keys, (((1,), (1,)), ((), ())), preferred_element_type=jnp.float32)
        if visible is not None:
            score = jnp.where(visible, score, NEGATIVE)
        before = m_ref[at]
        peak = jnp.maximum(before, jnp.max(score, axis=1, keepdims=True))
        fade = jnp.exp2((before - peak) * SCALE)
        weight = jnp.exp2((score - peak) * SCALE)
        m_ref[at] = peak
        l_ref[at] = l_ref[at] * fade + jnp.sum(weight, axis=1, keepdims=True)
        acc_ref[at] = acc_ref[at] * fade + jnp.dot(
            weight.astype(jnp.bfloat16), values, preferred_element_type=jnp.float32)


def planned(step):
    at = jnp.int32(-1)
    for when, what in O_PLAN:
        at = jnp.where(step == when, what, at)
    return at


def block_kernel(x_ref, wq_ref, wk_ref, wv_ref, wo_ref, pos_ref, freq_ref, gain_ref, out_ref,
                 hid, pos, freq, gain, aux, seen, wall, full, kv, oall, qs, m_ref, l_ref, acc, att,
                 part, xin, zout, zin, fin, tin, loc, snd, rcv, sib_s, sib_r, att_sem, x_s, x_r, z_s, z_r, t_s, t_r, *gsems):
    p = Place()
    core, chip = p.core, p.chip
    tok = x_ref.shape[0]
    sib = p.sibling()
    given = Inputs(p, x_ref, wq_ref, wk_ref, wv_ref, pos_ref, hid, pos, wall, loc, snd, rcv)
    o_own = pltpu.make_async_copy(wo_ref, oall.at[chip], loc.at[4])
    f_own = pltpu.make_async_copy(freq_ref, freq, loc.at[5])
    n_own = pltpu.make_async_copy(gain_ref, gain, loc.at[6])
    given.start(False)
    for c in (f_own, o_own, n_own):
        c.start()
    entry(p)
    given.start(True)
    n = len(gsems) // 3
    g_w = Gather(p, wall, 96, gsems[:n])
    g_o = Gather(p, oall, 48, gsems[n:2 * n])
    g_kv = Gather(p, kv.at[core], 192, gsems[2 * n:])
    given.wait(0, 1)
    g_w.begin()
    full[...] = jnp.zeros_like(full)

    given.wait(3)
    f_own.wait()
    sign = jnp.where(lax.broadcasted_iota(jnp.int32, (1, HD), 1) < HD // 2, -1.0, 1.0)
    for c in range(2):
        at = pl.ds(c * tok, tok)
        column = jnp.transpose(jnp.broadcast_to(pos[c].astype(jnp.float32), (tok, tok)))
        angle = column * freq[...]
        aux[at, 0:HD] = jnp.cos(angle)
        aux[at, HD:2 * HD] = jnp.sin(angle) * sign
        for k in range(2):
            seen[at, k * tok:(k + 1) * tok] = (pos[k].astype(jnp.float32) <= column).astype(jnp.float32)

    def project(t, _):
        pl.when(t < ROUNDS - 1)(lambda: g_w.round(t))
        @pl.when(t == O_BEGIN)
        def _():
            o_own.wait()
            g_o.begin()

        g_o.round(planned(t))
        d = t - USE_AT

        def use(g, _):
            @pl.when((g >= 0) & (g < ROWS))
            def _():
                row = g_w.row(g)
                g_w.line_arrived(row)
                depth = LINE * 128
                left = hid[:, pl.ds(pl.multiple_of(row * depth, depth), depth)]
                at = pl.ds(pl.multiple_of(row * LINE, LINE), LINE)
                full[...] += jnp.dot(left, wall[at].reshape(depth, wall.shape[2]), preferred_element_type=jnp.float32)
            return 0

        @pl.when(d == 0)
        def _():
            given.wait(2)

        @pl.when(d >= 0)
        def _():
            lax.fori_loop(2 * d - 1, 2 * d + 1, use, 0)

        pl.when(t == ROUNDS - 1)(lambda: g_w.others(ROWS - 1))
        return 0

    lax.fori_loop(0, STEPS, project, 0)

    cosine, sine = aux[:, 0:HD], aux[:, HD:2 * HD]
    last = full[:, 2 * HD:]
    kv[core, chip] = jnp.where(core == 0, turn(last, cosine, sine), last).astype(jnp.bfloat16)
    def relay(slots, sem, kind):
        ref = kv.at[kind, slots]
        return remote(ref, ref, sib_s.at[0], sib_r.at[sem], sib)

    relay(pl.ds(chip, 1), ROWS, core).start()
    g_kv.begin()
    for h in range(2):
        qs[pl.ds(2 * tok * h, 2 * tok)] = turn(full[:, h * HD:(h + 1) * HD], cosine, sine).astype(jnp.bfloat16)
    m_ref[...] = jnp.full_like(m_ref, NEGATIVE)
    l_ref[...] = jnp.zeros_like(l_ref)
    acc[...] = jnp.zeros_like(acc)

    def block(kind, start, count):
        return kv[kind, pl.ds(start, count)].reshape(count * 2 * tok, HD)

    def look(t, _):
        pl.when(t < ROUNDS - 1)(lambda: g_kv.round(t))
        g_o.round(planned(t + STEPS))
        d = t - USE_AT

        @pl.when(t == 0)
        def _():
            relay(pl.ds(chip, 1), ROWS, 1 - core).wait_recv()
            attend(qs, m_ref, l_ref, acc, block(0, chip, 1), block(1, chip, 1), seen[...] > 0.5)

        @pl.when(d == 0)
        def _():
            g_kv.line_arrived(p.y)
            for i in range(1, LINE):
                relay(pl.ds(p.y * LINE + p.order(i), 1), p.y, core).start()
            relay(pl.ds(0, LINE - 1), p.y, 1 - core).wait_recv()

            def one(z, _):
                slot = p.y * LINE + z
                attend(qs, m_ref, l_ref, acc, block(0, slot, 1), block(1, slot, 1))
                return 0
            lax.fori_loop(0, p.z, one, 0)

        def forward(g, _):
            @pl.when((g >= 1) & (g < ROWS))
            def _():
                row = g_kv.row(g)
                g_kv.line_arrived(row)
                relay(pl.ds(pl.multiple_of(row * LINE, LINE), LINE), row, core).start()
            return 0

        def use(g, _):
            @pl.when((g >= 1) & (g < ROWS))
            def _():
                row = g_kv.row(g)
                start = pl.multiple_of(row * LINE, LINE)
                relay(pl.ds(start, LINE), row, 1 - core).wait_recv()
                pl.when(row < p.y)(lambda: attend(qs, m_ref, l_ref, acc, block(0, start, LINE), block(1, start, LINE)))
            return 0

        @pl.when(d >= 1)
        def _():
            lax.fori_loop(2 * d - 1, 2 * d + 1, forward, 0)
            lax.fori_loop(2 * d - 1, 2 * d + 1, use, 0)

        pl.when(t == ROUNDS - 1)(lambda: g_kv.others(ROWS - 1))
        return 0

    lax.fori_loop(0, STEPS, look, 0)

    done = (acc[...] / l_ref[...]).astype(jnp.bfloat16)
    share = tok // 8
    for h in range(2):
        for xt in range(4):
            for zt in range(2):
                for c in range(2):
                    src = h * 2 * tok + c * tok + (zt * 4 + xt) * share
                    dst = (xt * 4 + zt * 2 + c) * share
                    att[core, dst:dst + share, h * HD:(h + 1) * HD] = done[src:src + share]
    swap = remote(att.at[core], att.at[core], att_sem.at[0], att_sem.at[1], sib)
    swap.start()
    swap.wait()

    span = LINE * 64
    piece = 4 * share
    wide_chunk = span

    def x_copies(c):
        cols = pl.ds(pl.multiple_of(c * wide_chunk, wide_chunk), wide_chunk)
        return [remote(part.at[(p.x + step) % 4, :, cols], xin.at[k, :, cols], x_s.at[0], x_r.at[k, c], p.across(step))
                for k, step in enumerate((2, 1, 3))]

    def keep(which):
        return pl.ds(pl.multiple_of(which * share, share), share)

    def z_copy(cols, to):
        return remote(zout.at[keep(to), cols], zin.at[core, :, cols], z_s.at[0], z_r.at[core], p.far(to))

    def t_copy(cols):
        return remote(fin.at[1 - core, :, cols], tin.at[:, cols], t_s.at[0], t_r.at[0], sib)

    def produce(g):
        r = g_o.row(g)
        at = pl.ds(pl.multiple_of(r * LINE, LINE), LINE)
        g_o.line_arrived(r)
        left = jnp.concatenate([att[0], att[1]], axis=1)
        prod = lax.dot_general(left, oall[at].reshape(span, oall.shape[2]), (((1,), (1,)), ((), ())),
                               preferred_element_type=jnp.float32)
        part[:, :, pl.ds(pl.multiple_of(g * span, span), span)] = prod.astype(jnp.bfloat16).reshape(4, piece, span)
        for cp in x_copies(g):
            cp.start()

    def merge(c):
        cols = pl.ds(pl.multiple_of(c * wide_chunk, wide_chunk), wide_chunk)
        for cp in x_copies(c):
            cp.wait_recv()
        half = piece // 2

        def summed(z):
            at = pl.ds(pl.multiple_of(z * half, half), half)
            f = lambda v: v.astype(jnp.float32)
            return f(part[p.x, at, cols]) + f(xin[0, at, cols]) + f(xin[1, at, cols]) + f(xin[2, at, cols])

        zout[:, cols] = summed(1 - p.zh).astype(jnp.bfloat16)
        z_copy(cols, core).start()
        z_copy(cols, 1 - core).start()
        fin[:, :, cols] = summed(p.zh).reshape(2, share, wide_chunk)
        t_copy(cols).start()

    chunks = ROWS

    def flow(s, _):
        pl.when(s < chunks)(lambda: produce(s))
        g_o.round(planned(s + 2 * STEPS))
        pl.when(s >= MERGE_AT)(lambda: merge(s - MERGE_AT))
        return 0

    lax.fori_loop(0, chunks + MERGE_AT, flow, 0)
    remote(tin, tin, t_s.at[0], t_r.at[0], sib).wait_recv()
    for k in range(2):
        remote(zin.at[k], zin.at[k], z_s.at[0], z_r.at[k], sib).wait_recv()
    mine = fin[core] + zin[core].astype(jnp.float32)
    theirs = tin[...] + zin[1 - core].astype(jnp.float32)
    even = jnp.where(core == 0, mine, theirs)
    odd = jnp.where(core == 0, theirs, mine)
    low = lax.broadcasted_iota(jnp.int32, (share, HD), 1) < HD // 2
    at = pl.ds(pl.multiple_of(core * tok + p.head * share, share), share)
    square = jnp.zeros((share, 1), jnp.float32)
    tiles = []
    for g in range(ROWS):
        for m in range(2):
            cut = g * span + m * HD
            a, b = even[:, cut:cut + HD], odd[:, cut:cut + HD]
            pair = (jnp.where(low, a, pltpu.roll(b, 64, 1)), jnp.where(low, pltpu.roll(a, 64, 1), b))
            for k in range(2):
                cols = pl.ds(pl.multiple_of(g_o.row(g) * 2 * span + (2 * m + k) * HD, HD), HD)
                value = pair[k] + hid[at, cols].astype(jnp.float32)
                square += jnp.sum(value * value, axis=1, keepdims=True)
                tiles.append((cols, value))
    n_own.wait()
    norm = lax.rsqrt(square * (1.0 / (CHIPS * HD)) + 1e-05)
    for cols, value in tiles:
        out_ref[:, cols] = (value * norm * gain[:, cols]).astype(jnp.bfloat16)

    g_w.drain()
    g_o.drain()
    g_kv.drain()

    remote(xin, xin, x_s.at[0], x_r.at[0, 0], p.across(1)).wait_send()

    remote(zout, zout, z_s.at[0], z_r.at[0], sib).wait_send()
    remote(tin, tin, t_s.at[0], t_r.at[0], sib).wait_send()
    relay(pl.ds(0, CHIPS), 0, core).wait_send()


def whole(x, wq, wk, wv, wo, pos, freq, gain):
    tok = x.shape[0]
    width = x.shape[1]
    dma = pltpu.SemaphoreType.DMA
    anyspec = pl.BlockSpec(memory_space=pl.ANY)
    vm = pl.BlockSpec(memory_space=pltpu.VMEM)
    bf, f32 = jnp.bfloat16, jnp.float32
    share = tok // 8
    half = width // 2
    return pl.pallas_call(
        block_kernel,
        out_shape=jax.ShapeDtypeStruct((share, width), bf),
        in_specs=[anyspec] * 8,
        out_specs=vm,
        scratch_shapes=[
            pltpu.VMEM((2 * tok, width), bf),
            pltpu.VMEM((2, 1, tok), jnp.int32),
            pltpu.VMEM((1, HD), f32),
            pltpu.VMEM((1, width), f32),
            pltpu.VMEM((2 * tok, 2 * HD), f32),
            pltpu.VMEM((2 * tok, 2 * tok), f32),
            pltpu.VMEM((CHIPS, 128, 384), bf),
            pltpu.VMEM((2 * tok, 384), f32),
            pltpu.VMEM((2, CHIPS, 2 * tok, HD), bf),
            pltpu.VMEM((CHIPS, 64, 512), bf),
            pltpu.VMEM((4 * tok, HD), bf),
            pltpu.VMEM((4 * tok, 1), f32),
            pltpu.VMEM((4 * tok, 1), f32),
            pltpu.VMEM((4 * tok, HD), f32),
            pltpu.VMEM((2, 2 * tok, 256), bf),
            pltpu.VMEM((4, 4 * share, half), bf),
            pltpu.VMEM((3, 4 * share, half), bf),
            pltpu.VMEM((2 * share, half), bf),
            pltpu.VMEM((2, share, half), bf),
            pltpu.VMEM((2, share, half), f32),
            pltpu.VMEM((share, half), f32),
            dma((7,)), dma((4,)), dma((4,)),
            dma((1,)), dma((ROWS + 1,)), dma((2,)),
            dma((1,)), dma((3, ROWS)), dma((1,)), dma((2,)), dma((1,)), dma((1,)),
        ] + Gather.scratch() * 3,
        compiler_params=pltpu.CompilerParams(collective_id=0, has_side_effects=True, vmem_limit_bytes=56 << 20),
        name="block",
    )(x, wq, wk, wv, wo, pos, freq, gain)


def on_device(hidden_in, positions, w_query, w_key, w_value, w_out, norm_gain):
    half = np.arange(HD // 2, dtype=np.float64)
    freq = jnp.asarray(np.tile(500000.0 ** (-2.0 * half / HD), 2).astype(np.float32).reshape(1, HD))
    return whole(hidden_in, w_query, w_key, w_value, w_out.T, positions.reshape(1, -1), freq, norm_gain.reshape(1, -1))


def solution(mesh):
    return jax.shard_map(
        on_device,
        mesh=mesh,
        in_specs=(P("ctx", None), P("ctx"), P("ctx", "head"), P("ctx", "head"), P("ctx", "head"), P("head", "ctx"), P()),
        out_specs=P(("ctx", "head"), None),
        check_vma=False,
    )
```

```python
import jax
import jax.numpy as jnp
from jax import lax
from jax.experimental import pallas as pl
from jax.experimental.pallas import tpu as pltpu
from jax.sharding import PartitionSpec as P
import numpy as np

MESH = pl.DeviceIdType.MESH
HD = 128
ROWS = 8
LINE = 4
CHIPS = ROWS * LINE
ROUNDS = ROWS // 2 + 2
USE_AT = 2
STEPS = ROUNDS + USE_AT - 1
O_BEGIN = 0
O_PLAN = ((4, 1), (12, 2), (13, 3), (14, 4), (16, 5))
MERGE_AT = 4
NEGATIVE = -1e30
SCALE = 1.4426950408889634 / HD ** 0.5


class Place:
    def __init__(self):
        ctx = lax.axis_index("ctx")
        head = lax.axis_index("head")
        self.core = ctx % 2
        self.z = (ctx // 2) % LINE
        self.y = ctx // (2 * LINE)
        self.x = head % 4
        self.zh = head // 4
        self.chip = ctx // 2
        self.ctx = ctx
        self.head = head

    def at(self, y, z, core):
        return ((y * LINE + z) * 2 + core, self.head)

    def sibling(self):
        return (self.chip * 2 + 1 - self.core, self.head)

    def up(self):
        return self.at((self.y + 1) % ROWS, self.z, self.core)

    def down(self):
        return self.at((self.y + ROWS - 1) % ROWS, self.z, self.core)

    def across(self, steps):
        return (self.ctx, self.zh * 4 + (self.x + 4 + steps) % 4)

    def far(self, core):
        return (self.chip * 2 + core, (1 - self.zh) * 4 + self.x)

    def order(self, i):
        z = self.z
        if i == 0:
            return z
        a = (1, 0, 3, 2)
        b = (2, 2, 1, 1)
        c = (3, 3, 0, 0)
        t = (a, b, c)[i - 1]
        return jnp.where(z == 0, t[0], jnp.where(z == 1, t[1], jnp.where(z == 2, t[2], t[3])))


class Gather:
    def __init__(self, place, buf, cut, sems):
        self.p = place
        self.buf, self.cut = buf, cut
        self.rf, self.ly, self.lz, self.out = sems

    @staticmethod
    def scratch():
        dma = pltpu.SemaphoreType.DMA
        return [dma((CHIPS,)), dma((ROWS,)), dma((ROWS,)), dma((1,))]

    def row(self, g):
        d = (g + 1) // 2
        up = jnp.logical_and(g % 2 == 1, jnp.logical_or(g < 7, self.p.core == 0))
        return jnp.where(up, self.p.y + ROWS - d, self.p.y + d) % ROWS

    def first(self, slot):
        return self.buf.at[slot, pl.ds(0, self.cut)]

    def last(self, slot):
        return self.buf.at[slot, pl.ds(self.cut, self.buf.shape[1] - self.cut)]

    def copy(self, ref, sem, device):
        return remote(ref, ref, self.out.at[0], sem, device)

    def onward(self, g):
        core = self.p.core
        return ((g == 1) | (g == 3) | ((g == 5) & (core == 0)),
                (g == 2) | (g == 4) | ((g == 6) & (core == 1)))

    def along(self, make, g):
        up, down = self.onward(g)

        @pl.when(up)
        def _():
            make(self.p.up()).start()

        @pl.when(down)
        def _():
            make(self.p.down()).start()

    def line(self, make):
        for i in range(1, LINE):
            make(self.p.at(self.p.y, self.p.order(i), self.p.core)).start()

    def begin(self):
        p = self.p
        slot = p.chip
        self.line(lambda dev: self.copy(self.first(slot), self.rf.at[slot], dev))
        for dev in (p.up(), p.down()):
            self.copy(self.last(slot), self.ly.at[p.y], dev).start()
            self.copy(self.first(slot), self.rf.at[slot], dev).start()
        self.line(lambda dev: self.copy(self.last(slot), self.lz.at[p.y], dev))

    def near(self, g):
        row = self.row(g)
        slot = row * LINE + self.p.z
        here = self.copy(self.last(slot), self.ly.at[row], self.p.up())
        here.wait_recv()
        self.along(lambda dev: self.copy(self.last(slot), self.ly.at[row], dev), g)
        self.line(lambda dev: self.copy(self.last(slot), self.lz.at[row], dev))
        self.pass_on(g, slot)

    def pass_on(self, g, slot):
        make = lambda dev: self.copy(self.first(slot), self.rf.at[slot], dev)
        make(self.p.up()).wait_recv()
        self.along(make, g)

    def others(self, g):
        row = self.row(g)
        for i in range(1, LINE):
            self.pass_on(g, row * LINE + self.p.order(i))

    def line_arrived(self, row):
        three = self.buf.at[pl.ds(0, LINE - 1), pl.ds(self.cut, self.buf.shape[1] - self.cut)]
        self.copy(three, self.lz.at[row], self.p.up()).wait_recv()

    def round(self, t):
        for g in (2 * t - 1, 2 * t):
            pl.when((g >= 1) & (g < ROWS))(lambda g=g: self.near(g))

        @pl.when(t == 1)
        def _():
            for i in range(1, LINE):
                slot = self.p.y * LINE + self.p.order(i)
                make = lambda dev: self.copy(self.first(slot), self.rf.at[slot], dev)
                make(self.p.up()).wait_recv()
                make(self.p.up()).start()
                make(self.p.down()).start()

        for g in (2 * t - 3, 2 * t - 2):
            pl.when((g >= 1) & (g < ROWS))(lambda g=g: self.others(g))

    def drain(self):
        sent = self.buf.at[pl.ds(0, CHIPS - 1)]
        self.copy(sent, self.ly.at[0], self.p.up()).wait_send()


def remote(src, dst, send, recv, device):
    return pltpu.make_async_remote_copy(
        src_ref=src, dst_ref=dst, send_sem=send, recv_sem=recv, device_id=device, device_id_type=MESH)


def entry(p):
    bar = pltpu.get_barrier_semaphore()
    devices = [p.far(p.core), p.far(1 - p.core), p.across(2)] + [p.at(p.y, p.order(i), p.core) for i in range(LINE - 1, 0, -1)]
    devices += [p.across(1), p.across(-1), p.up(), p.down(), p.sibling()]
    for d in devices:
        pl.semaphore_signal(bar, inc=1, device_id=d, device_id_type=MESH)
    pl.semaphore_wait(bar, len(devices))


class Inputs:
    def __init__(self, p, x_ref, wq_ref, wk_ref, wv_ref, pos_ref, hid, pos, wall, loc, snd, rcv):
        core = p.core
        tok = x_ref.shape[0]
        depth = wq_ref.shape[0]
        half = wq_ref.shape[1] // 2
        columns = lambda c: pl.ds(pl.multiple_of(c * half, half), half)
        span = pl.ds(pl.multiple_of(core * depth, depth), depth)
        rows = pl.ds(pl.multiple_of(core * tok, tok), tok)
        slot_q = wall.at[p.chip, span, pl.ds(0, half)]
        slot_l = wall.at[p.chip, span, pl.ds(half, HD)]
        self.core = core
        self.narrow = (wk_ref, wv_ref)
        self.local = lambda ref, dst, k: pltpu.make_async_copy(ref, dst, loc.at[k])
        self.cross = lambda ref, dst, k: remote(ref, dst, snd.at[k], rcv.at[k], p.sibling())
        self.slot_l = slot_l
        pairs = ((wq_ref.at[:, columns(core)], wq_ref.at[:, columns(1 - core)], slot_q), None,
                 (x_ref, x_ref, hid.at[rows]), (pos_ref, pos_ref, pos.at[core]))
        self.own = [self.local(q[0], q[2], k) if q else self.local(wk_ref, slot_l, 1) for k, q in enumerate(pairs)]
        self.sent = [self.cross(q[1], q[2], k) if q else self.cross(wk_ref, slot_l, 1) for k, q in enumerate(pairs)]

    def start(self, far):
        make = self.cross if far else self.local
        for c in range(2):
            kept = self.narrow[1 - c if far else c]
            pl.when(self.core == c)(lambda kept=kept: make(kept, self.slot_l, 1).start())
        for k in (0, 3, 2):
            (self.sent if far else self.own)[k].start()

    def wait(self, *ks):
        for k in ks:
            self.own[k].wait()
            self.sent[k].wait_send()
            self.sent[k].wait_recv()


def turn(u, cosine, sine):
    return u * cosine + pltpu.roll(u, 64, 1) * sine


def attend(q_ref, m_ref, l_ref, acc_ref, keys, values, visible=None):
    rows = q_ref.shape[0] // 2
    for h in range(2):
        at = pl.ds(h * rows, rows)
        score = lax.dot_general(q_ref[at], keys, (((1,), (1,)), ((), ())), preferred_element_type=jnp.float32)
        if visible is not None:
            score = jnp.where(visible, score, NEGATIVE)
        before = m_ref[at]
        peak = jnp.maximum(before, jnp.max(score, axis=1, keepdims=True))
        fade = jnp.exp2((before - peak) * SCALE)
        weight = jnp.exp2((score - peak) * SCALE)
        m_ref[at] = peak
        l_ref[at] = l_ref[at] * fade + jnp.sum(weight, axis=1, keepdims=True)
        acc_ref[at] = acc_ref[at] * fade + jnp.dot(
            weight.astype(jnp.bfloat16), values, preferred_element_type=jnp.float32)


def planned(step):
    at = jnp.int32(-1)
    for when, what in O_PLAN:
        at = jnp.where(step == when, what, at)
    return at


def block_kernel(x_ref, wq_ref, wk_ref, wv_ref, wo_ref, pos_ref, freq_ref, gain_ref, out_ref,
                 hid, pos, freq, gain, aux, seen, wall, full, kv, oall, qs, m_ref, l_ref, acc, att,
                 part, xin, zout, zin, fin, tin, loc, snd, rcv, sib_s, sib_r, att_sem, x_s, x_r, z_s, z_r, t_s, t_r, *gsems):
    p = Place()
    core, chip = p.core, p.chip
    tok = x_ref.shape[0]
    sib = p.sibling()
    given = Inputs(p, x_ref, wq_ref, wk_ref, wv_ref, pos_ref, hid, pos, wall, loc, snd, rcv)
    o_own = pltpu.make_async_copy(wo_ref, oall.at[chip], loc.at[4])
    f_own = pltpu.make_async_copy(freq_ref, freq, loc.at[5])
    n_own = pltpu.make_async_copy(gain_ref, gain, loc.at[6])
    given.start(False)
    for c in (f_own, o_own, n_own):
        c.start()
    entry(p)
    given.start(True)
    n = len(gsems) // 3
    g_w = Gather(p, wall, 96, gsems[:n])
    g_o = Gather(p, oall, 48, gsems[n:2 * n])
    g_kv = Gather(p, kv.at[core], 192, gsems[2 * n:])
    given.wait(0, 1)
    g_w.begin()
    full[...] = jnp.zeros_like(full)

    given.wait(3)
    f_own.wait()
    sign = jnp.where(lax.broadcasted_iota(jnp.int32, (1, HD), 1) < HD // 2, -1.0, 1.0)
    for c in range(2):
        at = pl.ds(c * tok, tok)
        column = jnp.transpose(jnp.broadcast_to(pos[c].astype(jnp.float32), (tok, tok)))
        angle = column * freq[...]
        aux[at, 0:HD] = jnp.cos(angle)
        aux[at, HD:2 * HD] = jnp.sin(angle) * sign
        for k in range(2):
            seen[at, k * tok:(k + 1) * tok] = (pos[k].astype(jnp.float32) <= column).astype(jnp.float32)

    def project(t, _):
        pl.when(t < ROUNDS - 1)(lambda: g_w.round(t))
        @pl.when(t == O_BEGIN)
        def _():
            o_own.wait()
            g_o.begin()

        g_o.round(planned(t))
        d = t - USE_AT

        def use(g, _):
            @pl.when((g >= 0) & (g < ROWS))
            def _():
                row = g_w.row(g)
                g_w.line_arrived(row)
                depth = LINE * 128
                left = hid[:, pl.ds(pl.multiple_of(row * depth, depth), depth)]
                at = pl.ds(pl.multiple_of(row * LINE, LINE), LINE)
                full[...] += jnp.dot(left, wall[at].reshape(depth, wall.shape[2]), preferred_element_type=jnp.float32)
            return 0

        @pl.when(d == 0)
        def _():
            given.wait(2)

        @pl.when(d >= 0)
        def _():
            lax.fori_loop(2 * d - 1, 2 * d + 1, use, 0)

        pl.when(t == ROUNDS - 1)(lambda: g_w.others(ROWS - 1))
        return 0

    lax.fori_loop(0, STEPS, project, 0)

    cosine, sine = aux[:, 0:HD], aux[:, HD:2 * HD]
    last = full[:, 2 * HD:]
    kv[core, chip] = jnp.where(core == 0, turn(last, cosine, sine), last).astype(jnp.bfloat16)
    def relay(slots, sem, kind):
        ref = kv.at[kind, slots]
        return remote(ref, ref, sib_s.at[0], sib_r.at[sem], sib)

    relay(pl.ds(chip, 1), ROWS, core).start()
    g_kv.begin()
    for h in range(2):
        qs[pl.ds(2 * tok * h, 2 * tok)] = turn(full[:, h * HD:(h + 1) * HD], cosine, sine).astype(jnp.bfloat16)
    m_ref[...] = jnp.full_like(m_ref, NEGATIVE)
    l_ref[...] = jnp.zeros_like(l_ref)
    acc[...] = jnp.zeros_like(acc)

    def block(kind, start, count):
        return kv[kind, pl.ds(start, count)].reshape(count * 2 * tok, HD)

    def look(t, _):
        pl.when(t < ROUNDS - 1)(lambda: g_kv.round(t))
        g_o.round(planned(t + STEPS))
        d = t - USE_AT

        @pl.when(t == 0)
        def _():
            relay(pl.ds(chip, 1), ROWS, 1 - core).wait_recv()
            attend(qs, m_ref, l_ref, acc, block(0, chip, 1), block(1, chip, 1), seen[...] > 0.5)

        @pl.when(d == 0)
        def _():
            g_kv.line_arrived(p.y)
            for i in range(1, LINE):
                relay(pl.ds(p.y * LINE + p.order(i), 1), p.y, core).start()
            relay(pl.ds(0, LINE - 1), p.y, 1 - core).wait_recv()

            def one(z, _):
                slot = p.y * LINE + z
                attend(qs, m_ref, l_ref, acc, block(0, slot, 1), block(1, slot, 1))
                return 0
            lax.fori_loop(0, p.z, one, 0)

        def forward(g, _):
            @pl.when((g >= 1) & (g < ROWS))
            def _():
                row = g_kv.row(g)
                g_kv.line_arrived(row)
                relay(pl.ds(pl.multiple_of(row * LINE, LINE), LINE), row, core).start()
            return 0

        def use(g, _):
            @pl.when((g >= 1) & (g < ROWS))
            def _():
                row = g_kv.row(g)
                start = pl.multiple_of(row * LINE, LINE)
                relay(pl.ds(start, LINE), row, 1 - core).wait_recv()
                pl.when(row < p.y)(lambda: attend(qs, m_ref, l_ref, acc, block(0, start, LINE), block(1, start, LINE)))
            return 0

        @pl.when(d >= 1)
        def _():
            lax.fori_loop(2 * d - 1, 2 * d + 1, forward, 0)
            lax.fori_loop(2 * d - 1, 2 * d + 1, use, 0)

        pl.when(t == ROUNDS - 1)(lambda: g_kv.others(ROWS - 1))
        return 0

    lax.fori_loop(0, STEPS, look, 0)

    done = (acc[...] / l_ref[...]).astype(jnp.bfloat16)
    share = tok // 8
    for h in range(2):
        for xt in range(4):
            for zt in range(2):
                for c in range(2):
                    src = h * 2 * tok + c * tok + (zt * 4 + xt) * share
                    dst = (xt * 4 + zt * 2 + c) * share
                    att[core, dst:dst + share, h * HD:(h + 1) * HD] = done[src:src + share]
    swap = remote(att.at[core], att.at[core], att_sem.at[0], att_sem.at[1], sib)
    swap.start()
    swap.wait()

    span = LINE * 64
    piece = 4 * share
    wide_chunk = span

    def x_copies(c):
        cols = pl.ds(pl.multiple_of(c * wide_chunk, wide_chunk), wide_chunk)
        return [remote(part.at[(p.x + step) % 4, :, cols], xin.at[k, :, cols], x_s.at[0], x_r.at[k, c], p.across(step))
                for k, step in enumerate((2, 1, 3))]

    def keep(which):
        return pl.ds(pl.multiple_of(which * share, share), share)

    def z_copy(cols, to):
        return remote(zout.at[keep(to), cols], zin.at[core, :, cols], z_s.at[0], z_r.at[core], p.far(to))

    def t_copy(cols):
        return remote(fin.at[1 - core, :, cols], tin.at[:, cols], t_s.at[0], t_r.at[0], sib)

    def produce(g):
        r = g_o.row(g)
        at = pl.ds(pl.multiple_of(r * LINE, LINE), LINE)
        g_o.line_arrived(r)
        left = jnp.concatenate([att[0], att[1]], axis=1)
        prod = lax.dot_general(left, oall[at].reshape(span, oall.shape[2]), (((1,), (1,)), ((), ())),
                               preferred_element_type=jnp.float32)
        part[:, :, pl.ds(pl.multiple_of(g * span, span), span)] = prod.astype(jnp.bfloat16).reshape(4, piece, span)
        for cp in x_copies(g):
            cp.start()

    def merge(c):
        cols = pl.ds(pl.multiple_of(c * wide_chunk, wide_chunk), wide_chunk)
        for cp in x_copies(c):
            cp.wait_recv()
        half = piece // 2

        def summed(z):
            at = pl.ds(pl.multiple_of(z * half, half), half)
            f = lambda v: v.astype(jnp.float32)
            return f(part[p.x, at, cols]) + f(xin[0, at, cols]) + f(xin[1, at, cols]) + f(xin[2, at, cols])

        zout[:, cols] = summed(1 - p.zh).astype(jnp.bfloat16)
        z_copy(cols, core).start()
        z_copy(cols, 1 - core).start()
        fin[:, :, cols] = summed(p.zh).reshape(2, share, wide_chunk)
        t_copy(cols).start()

    chunks = ROWS

    def flow(s, _):
        pl.when(s < chunks)(lambda: produce(s))
        g_o.round(planned(s + 2 * STEPS))
        pl.when(s >= MERGE_AT)(lambda: merge(s - MERGE_AT))
        return 0

    lax.fori_loop(0, chunks + MERGE_AT, flow, 0)
    remote(tin, tin, t_s.at[0], t_r.at[0], sib).wait_recv()
    for k in range(2):
        remote(zin.at[k], zin.at[k], z_s.at[0], z_r.at[k], sib).wait_recv()
    mine = fin[core] + zin[core].astype(jnp.float32)
    theirs = tin[...] + zin[1 - core].astype(jnp.float32)
    even = jnp.where(core == 0, mine, theirs)
    odd = jnp.where(core == 0, theirs, mine)
    low = lax.broadcasted_iota(jnp.int32, (share, HD), 1) < HD // 2
    at = pl.ds(pl.multiple_of(core * tok + p.head * share, share), share)
    square = jnp.zeros((share, 1), jnp.float32)
    tiles = []
    for g in range(ROWS):
        for m in range(2):
            cut = g * span + m * HD
            a, b = even[:, cut:cut + HD], odd[:, cut:cut + HD]
            pair = (jnp.where(low, a, pltpu.roll(b, 64, 1)), jnp.where(low, pltpu.roll(a, 64, 1), b))
            for k in range(2):
                cols = pl.ds(pl.multiple_of(g_o.row(g) * 2 * span + (2 * m + k) * HD, HD), HD)
                value = pair[k] + hid[at, cols].astype(jnp.float32)
                square += jnp.sum(value * value, axis=1, keepdims=True)
                tiles.append((cols, value))
    n_own.wait()
    norm = lax.rsqrt(square * (1.0 / (CHIPS * HD)) + 1e-05)
    for cols, value in tiles:
        out_ref[:, cols] = (value * norm * gain[:, cols]).astype(jnp.bfloat16)

    g_w.drain()
    g_o.drain()
    g_kv.drain()

    remote(xin, xin, x_s.at[0], x_r.at[0, 0], p.across(1)).wait_send()

    remote(zout, zout, z_s.at[0], z_r.at[0], sib).wait_send()
    remote(tin, tin, t_s.at[0], t_r.at[0], sib).wait_send()
    relay(pl.ds(0, CHIPS), 0, core).wait_send()


def whole(x, wq, wk, wv, wo, pos, freq, gain):
    tok = x.shape[0]
    width = x.shape[1]
    dma = pltpu.SemaphoreType.DMA
    anyspec = pl.BlockSpec(memory_space=pl.ANY)
    vm = pl.BlockSpec(memory_space=pltpu.VMEM)
    bf, f32 = jnp.bfloat16, jnp.float32
    share = tok // 8
    half = width // 2
    return pl.pallas_call(
        block_kernel,
        out_shape=jax.ShapeDtypeStruct((share, width), bf),
        in_specs=[anyspec] * 8,
        out_specs=vm,
        scratch_shapes=[
            pltpu.VMEM((2 * tok, width), bf),
            pltpu.VMEM((2, 1, tok), jnp.int32),
            pltpu.VMEM((1, HD), f32),
            pltpu.VMEM((1, width), f32),
            pltpu.VMEM((2 * tok, 2 * HD), f32),
            pltpu.VMEM((2 * tok, 2 * tok), f32),
            pltpu.VMEM((CHIPS, 128, 384), bf),
            pltpu.VMEM((2 * tok, 384), f32),
            pltpu.VMEM((2, CHIPS, 2 * tok, HD), bf),
            pltpu.VMEM((CHIPS, 64, 512), bf),
            pltpu.VMEM((4 * tok, HD), bf),
            pltpu.VMEM((4 * tok, 1), f32),
            pltpu.VMEM((4 * tok, 1), f32),
            pltpu.VMEM((4 * tok, HD), f32),
            pltpu.VMEM((2, 2 * tok, 256), bf),
            pltpu.VMEM((4, 4 * share, half), bf),
            pltpu.VMEM((3, 4 * share, half), bf),
            pltpu.VMEM((2 * share, half), bf),
            pltpu.VMEM((2, share, half), bf),
            pltpu.VMEM((2, share, half), f32),
            pltpu.VMEM((share, half), f32),
            dma((7,)), dma((4,)), dma((4,)),
            dma((1,)), dma((ROWS + 1,)), dma((2,)),
            dma((1,)), dma((3, ROWS)), dma((1,)), dma((2,)), dma((1,)), dma((1,)),
        ] + Gather.scratch() * 3,
        compiler_params=pltpu.CompilerParams(collective_id=0, has_side_effects=True, vmem_limit_bytes=56 << 20),
        name="block",
    )(x, wq, wk, wv, wo, pos, freq, gain)


def on_device(hidden_in, positions, w_query, w_key, w_value, w_out, norm_gain):
    half = np.arange(HD // 2, dtype=np.float64)
    freq = jnp.asarray(np.tile(500000.0 ** (-2.0 * half / HD), 2).astype(np.float32).reshape(1, HD))
    return whole(hidden_in, w_query, w_key, w_value, w_out.T, positions.reshape(1, -1), freq, norm_gain.reshape(1, -1))


def solution(mesh):
    return jax.shard_map(
        on_device,
        mesh=mesh,
        in_specs=(P("ctx", None), P("ctx"), P("ctx", "head"), P("ctx", "head"), P("ctx", "head"), P("head", "ctx"), P()),
        out_specs=P(("ctx", "head"), None),
        check_vma=False,
    )
```
